32 devices in a mesh: span: 4 (over y, x), stream: 8 (over z, core).
Axes of the slice: x: 2, y: 2, z: 4, core: 2. Of those that a mesh axis runs over, the one named last changes fastest.
Arguments:
- state: float32 [6, 64, 16384], P(None, None, ('span', 'stream')), may hold values from -6 to 6
- stiffness: float32 [16384], P(('span', 'stream')), may hold values from 0.3 to 6
- crossing: int32 [2, 4096], P(None, ('span', 'stream')), may hold values from 0 to 511, as said below
- contact_send: int32 [2, 4, 32768], P(None, None, ('span', 'stream')), may hold values from 0 to 32767
- contact_recv: int32 [2, 4, 32768], P(None, None, ('span', 'stream')), may hold values from 0 to 32767
- contact_fill: int32 [2, 4, 256], P(None, None, ('span', 'stream')), may hold values from 0 to 128, as said below
Outputs:
- final_state: float32 [6, 64, 16384], P(None, None, ('span', 'stream'))
The draws below stay inside these ranges and needn't reach their ends.
Inputs may be any that keep to these rules, and one draw needn't show every extreme that they name: `crossing`: each slab's 2 * 64 entries of one step are distinct and include slots 0 and 511. `contact_fill`: in each run of 8 blocks the live blocks come first; all full except the last live one; some runs have every block live.
All inputs are finite; a program needn't handle non-finite values.
Results may differ from the reference program's by a relative error of at most 0.0001.
Values sent between devices are 32-bit elements; how exact they have to be, the bound alone decides.
A program may use at most 128 MiB of HBM per device.

```python
import math
import jax
import jax.numpy as jnp
from jax import lax

NODES = 64
FIELDS = 6
STEPS = 2
F_DEV = 512
M = 64
CB = 8
FIBRES = 16384
N_SPAN = 4
N_STREAM = 8


def draw_crossing(key, part):
    ndev = N_SPAN * N_STREAM
    keys = jax.random.split(key, STEPS * ndev)

    def single(subkey):
        inner = jax.random.permutation(subkey, F_DEV - 2) + 1
        listed = jnp.concatenate([jnp.array([0, F_DEV - 1], dtype=jnp.int32), inner[:2 * M - 2].astype(jnp.int32)])
        return jax.random.permutation(jax.random.fold_in(subkey, 7), listed)
    return jax.vmap(single)(keys).reshape(STEPS, ndev * 2 * M).astype(jnp.int32)


def draw_contact_fill(key, part):
    ndev = N_SPAN * N_STREAM
    shape = (STEPS, N_SPAN, ndev)
    livecount = jax.random.randint(jax.random.fold_in(key, 11), shape, 0, CB + 1)
    flat_pos = jnp.arange(STEPS * N_SPAN * ndev, dtype=jnp.int32).reshape(shape)
    livecount = jnp.where(flat_pos == 0, CB, livecount)
    lastfill = jax.random.randint(jax.random.fold_in(key, 12), shape, 1, 129)
    block = jnp.arange(CB, dtype=jnp.int32)
    full = block[None, None, None, :] < livecount[..., None] - 1
    last = block[None, None, None, :] == livecount[..., None] - 1
    fill = jnp.where(full, 128, jnp.where(last, lastfill[..., None], 0))
    return fill.reshape(STEPS, N_SPAN, ndev * CB).astype(jnp.int32)


def plant(drawn, rng, least, top_value):
    longest = drawn.shape.index(max(drawn.shape))
    spots = []
    for shift in (0, 1):
        where = [jax.random.randint(jax.random.fold_in(rng, axis), (), 0, length) for axis, length in enumerate(drawn.shape)]
        where[longest] = (where[longest] + shift) % drawn.shape[longest]
        spots.append(tuple(where))
    return drawn.at[spots[0]].set(least).at[spots[1]].set(top_value)


def block_levels(stream_key, dims, shards, low, top_value):
    gain, own = 1.0, jax.random.fold_in(stream_key, 6)
    for axis_at, blocks in shards:
        heights = jnp.exp(jax.random.uniform(jax.random.fold_in(own, axis_at), (blocks,), jnp.float32, low / len(shards), top_value / len(shards)))
        gain = gain * jnp.repeat(heights, dims[axis_at] // blocks).reshape([-1 if axis == axis_at else 1 for axis in range(len(dims))])
    return gain


def centred(stream_key, dims, spread, bound, cuts=(), held_as=jnp.bfloat16):
    values = spread * jax.random.normal(stream_key, dims, jnp.float32)
    if cuts:
        values = values * block_levels(stream_key, dims, cuts, -0.22, 0.18)
    return jnp.clip(values, -bound, bound).astype(held_as)


def setup_inputs(seed: int = 0) -> dict:
    streams_of = jax.random.split(jax.random.key(seed), 7)
    state = centred(streams_of[0], (FIELDS, NODES, FIBRES), 1.0, 6.0, ((2, 32),), jnp.float32)
    stiffness = jnp.clip(jnp.exp(math.log(6.0) - 2.9957322 * jax.random.uniform(streams_of[1], (FIBRES,), jnp.float32) ** block_levels(streams_of[1], (FIBRES,), ((0, 32),), -0.2, 0.2)), 0.3, 6.0)
    crossing = draw_crossing(jax.random.fold_in(streams_of[6], 71), 0)
    contact_send = plant(jax.random.randint(streams_of[3], (STEPS, N_SPAN, CB * 128 * N_SPAN * N_STREAM), 0, NODES * F_DEV), jax.random.fold_in(streams_of[3], 1), 0, (NODES * F_DEV) - 1).astype(jnp.int32)
    contact_recv = plant(jax.random.randint(streams_of[4], (STEPS, N_SPAN, CB * 128 * N_SPAN * N_STREAM), 0, NODES * F_DEV), jax.random.fold_in(streams_of[4], 1), 0, (NODES * F_DEV) - 1).astype(jnp.int32)
    contact_fill = draw_contact_fill(jax.random.fold_in(streams_of[6], 71), 0)
    return dict(state=state, stiffness=stiffness, crossing=crossing, contact_send=contact_send, contact_recv=contact_recv, contact_fill=contact_fill)


def thomas(coef, rhs):
    count = rhs.shape[1]
    first = 1.0 + coef
    cps = [-coef / first]
    ds = [rhs[:, 0] / first]
    for node in range(1, count):
        diag = 1.0 + coef if node == count - 1 else 1.0 + 2.0 * coef
        denom = diag + coef * cps[-1]
        cps.append(-coef / denom)
        ds.append((rhs[:, node] + coef * ds[-1]) / denom)
    outs = [ds[-1]]
    for node in range(count - 2, -1, -1):
        outs.append(ds[node] - cps[node] * outs[-1])
    return jnp.stack(outs[::-1], axis=1)


def take_cols(flat, index):
    return flat[:, index]


def reference(state, stiffness, crossing, contact_send, contact_recv, contact_fill):
    ndev = N_SPAN * N_STREAM
    fdev = state.shape[2] // ndev
    nodes = state.shape[1]
    fields = state.shape[0]
    quota = contact_send.shape[2] // ndev
    blocks = quota // 128
    half = crossing.shape[1] // ndev // 2
    xcur = state.reshape(fields, nodes, ndev, fdev).transpose(2, 0, 1, 3)
    coef = stiffness.reshape(ndev, fdev)
    for step in range(STEPS):
        pflat = xcur[:, :3].reshape(ndev, 3, nodes * fdev)
        sidx = contact_send[step].reshape(N_SPAN, ndev, quota).transpose(1, 0, 2)
        sent = jax.vmap(take_cols)(pflat, sidx)
        sent = sent.reshape(N_SPAN, N_STREAM, 3, N_SPAN, quota).transpose(3, 1, 0, 2, 4).reshape(ndev, N_SPAN, 3, quota)
        fill = contact_fill[step].reshape(N_SPAN, ndev, blocks).transpose(1, 0, 2)
        fill = fill.reshape(N_SPAN, N_STREAM, N_SPAN, blocks).transpose(2, 1, 0, 3).reshape(ndev, N_SPAN, blocks)
        live = (jnp.arange(128, dtype=jnp.int32)[None, None, None, :] < fill[..., None]).reshape(ndev, N_SPAN, quota)
        ridx = contact_recv[step].reshape(N_SPAN, ndev, quota).transpose(1, 0, 2)
        local = jax.vmap(take_cols)(pflat, ridx).transpose(0, 2, 1, 3)
        delta = sent - local
        radius = jnp.sum(delta * delta, axis=2, keepdims=True)
        force = jnp.where(live[:, :, None, :], 1.0 * delta / (1.0 + radius), 0.0)

        def gather_force(index, value):
            zero = jnp.zeros((3, nodes * fdev), value.dtype)
            return zero.at[:, index.reshape(-1)].add(value.transpose(1, 0, 2).reshape(3, -1))

        contact = jax.vmap(gather_force)(ridx, force).reshape(ndev, 3, nodes, fdev)
        rhs = jnp.concatenate([xcur[:, :3] + 0.5 * contact, xcur[:, 3:]], axis=1)
        solved = lax.map(lambda pair: thomas(pair[1], pair[0]), (rhs, coef))
        cross = crossing[step].reshape(ndev, 2 * half)
        slots_up = cross[:, :half]
        slots_down = cross[:, half:]
        pick = jax.vmap(lambda u, a: u[:, :, a])
        pick_c = jax.vmap(lambda u, a: u[a])
        shape5 = (N_SPAN, N_STREAM, fields, nodes, half)
        arrive_up = jnp.roll(pick(solved, slots_up).reshape(shape5), 1, axis=1).reshape(ndev, fields, nodes, half)
        arrive_down = jnp.roll(pick(solved, slots_down).reshape(shape5), -1, axis=1).reshape(ndev, fields, nodes, half)
        coef_up = jnp.roll(pick_c(coef, slots_up).reshape(N_SPAN, N_STREAM, half), 1, axis=1).reshape(ndev, half)
        coef_down = jnp.roll(pick_c(coef, slots_down).reshape(N_SPAN, N_STREAM, half), -1, axis=1).reshape(ndev, half)
        xcur = jax.vmap(lambda u, a, b, p, q: u.at[:, :, a].set(p).at[:, :, b].set(q))(solved, slots_up, slots_down, arrive_up, arrive_down)
        coef = jax.vmap(lambda u, a, b, p, q: u.at[a].set(p).at[b].set(q))(coef, slots_up, slots_down, coef_up, coef_down)
    return xcur.transpose(1, 2, 0, 3).reshape(fields, nodes, ndev * fdev)
```

```python
import functools
import math

import jax
import jax.numpy as jnp
import ml_dtypes
import numpy as np
from jax import lax
from jax.experimental import pallas as pl
from jax.experimental.pallas import tpu as pltpu
from jax.sharding import PartitionSpec as P

STEPS = 2
MESH = pl.DeviceIdType.MESH
F32 = jnp.float32
BF16 = jnp.bfloat16
LANES = 128
HALF_SLOTS = 256
SUB = 256


def cosine_tables(nodes):
    k = np.arange(nodes)[:, None]
    n = np.arange(nodes)[None, :]
    basis = np.sqrt(2.0 / nodes) * np.cos(np.pi * (n + 0.5) * k / nodes)
    basis[0] /= math.sqrt(2.0)

    def stacked(matrix):
        high = matrix.astype(ml_dtypes.bfloat16)
        low = (matrix - high.astype(np.float64)).astype(ml_dtypes.bfloat16)
        return np.concatenate([high, high, low], axis=1)

    lam = 2.0 - 2.0 * np.cos(np.pi * np.arange(nodes) / nodes)
    lam = np.repeat(lam[:, None], LANES, axis=1).astype(np.float32)
    return stacked(basis), stacked(basis.T), lam


def split(x):
    high = x.astype(BF16)
    return high, (x - high.astype(F32)).astype(BF16)


def split3(x):
    high, rest = x.astype(BF16), None
    rest = x - high.astype(F32)
    mid = rest.astype(BF16)
    return high, mid, (rest - mid.astype(F32)).astype(BF16)


def dot(a, b):
    return jnp.dot(a, b, preferred_element_type=F32)


def dot_nt(a, b):
    return lax.dot_general(a, b, (((1,), (1,)), ((), ())), preferred_element_type=F32)


def along_nodes(matrix, block):
    high, low = split(block)
    return dot(matrix, jnp.concatenate([high, low, high], axis=0))


def tall(row, rows):
    tile = jnp.broadcast_to(row, (16, row.shape[1])).astype(BF16)
    return jnp.concatenate([tile] * (rows // 16), axis=0)


def kernel(
    groups, n_stream,
    state, coef0, crossing, csend, crecv, cfill, fwd, inv, lam, iota,
    out,
    xh, parts, hot, local, acc, scale, coef_in, coef_out, sbuf, rbuf, mout, min_,
    c_send, c_recv, p_send, p_recv, m_send, m_recv,
):
    fields, nodes, fdev = state.shape
    quota = csend.shape[2]
    cross = crossing.shape[1]
    half = cross // 2
    npos = 3 * nodes
    rows = fields * nodes
    i = lax.axis_index("span")
    j = lax.axis_index("stream")
    down_dev = (i, lax.rem(j + 1, n_stream))
    up_dev = (i, lax.rem(j + n_stream - 1, n_stream))

    def mod(v):
        return lax.rem(v, groups)

    barrier = pltpu.get_barrier_semaphore()
    for dev in (down_dev, up_dev):
        pl.semaphore_signal(barrier, inc=1, device_id=dev, device_id_type=MESH)
    for k in range(1, groups):
        pl.semaphore_signal(
            barrier, inc=1, device_id=(mod(i + k), j), device_id_type=MESH
        )
    pl.semaphore_wait(barrier, groups + 1)

    lane = lax.broadcasted_iota(jnp.int32, (1, LANES), 1)
    node_iota = lax.broadcasted_iota(jnp.int32, (nodes, SUB), 0)

    def slot_hot(slot, q):
        pieces = []
        for part in range(fdev // HALF_SLOTS):
            rel = slot - part * HALF_SLOTS
            inside = (rel >= 0) & (rel < HALF_SLOTS)
            val = jnp.where(inside, rel, -1).astype(F32)
            wide = jnp.concatenate([iota[...]] * (q // LANES), axis=1)
            same = wide == tall(val, HALF_SLOTS)
            pieces.append(jnp.where(same, BF16(1), BF16(0)))
        return jnp.concatenate(pieces, axis=0)

    def gather(index, keep_at=None, sub=0):
        slot = lax.rem(index, fdev)
        node = lax.div(index, fdev)
        table = slot_hot(slot, SUB)
        if keep_at is not None:
            hot[keep_at, :, sub * SUB : (sub + 1) * SUB] = table
        picked = dot(parts[...], table)
        picked = picked[:npos] + picked[npos:]
        mask = node_iota == node
        return [
            jnp.sum(
                jnp.where(mask, picked[c * nodes : (c + 1) * nodes], 0.0),
                axis=0, keepdims=True,
            )
            for c in range(3)
        ]

    def set_parts(c, block):
        high, low = split(block)
        parts[c * nodes : (c + 1) * nodes, :] = high
        parts[npos + c * nodes : npos + (c + 1) * nodes, :] = low

    cross_hot = [slot_hot(crossing[s : s + 1, :], cross) for s in range(STEPS)]
    ones = jnp.ones((16, cross), BF16)
    keeps = [1.0 - dot_nt(ones, t)[:1] for t in cross_hot]

    coef = coef0[...]
    wide_coef = jnp.broadcast_to(coef, (16, fdev))
    leaving = sum(dot(p, cross_hot[0]) for p in split3(wide_coef))
    coef_out[...] = leaving[:8]
    coef_copies = [
        pltpu.make_async_remote_copy(
            src_ref=coef_out, dst_ref=coef_in.at[d],
            send_sem=c_send.at[d], recv_sem=c_recv.at[d],
            device_id=dev, device_id_type=MESH,
        )
        for d, dev in enumerate((down_dev, up_dev))
    ]
    for copy in coef_copies:
        copy.start()

    def set_scale(c):
        for b in range(fdev // LANES):
            at = slice(b * LANES, (b + 1) * LANES)
            scale[:, at] = 1.0 / (1.0 + lam[...] * c[:, at])

    def pair_copy(step, k):
        to = mod(i + 1 + k)
        return pltpu.make_async_remote_copy(
            src_ref=sbuf.at[step, to], dst_ref=rbuf.at[step, i],
            send_sem=p_send.at[step, to], recv_sem=p_recv.at[step, i],
            device_id=(to, j), device_id_type=MESH,
        )

    def pair_arrival(step, source):
        return pltpu.make_async_remote_copy(
            src_ref=sbuf.at[step, source], dst_ref=rbuf.at[step, source],
            send_sem=p_send.at[step, source], recv_sem=p_recv.at[step, source],
            device_id=(source, j), device_id_type=MESH,
        )

    for c in range(3):
        set_parts(c, state[c])

    for step in range(STEPS):

        def send_gather(g, buf):
            fill = cfill[step, pl.ds(g, 1), :]
            for sub in range(quota // SUB):
                at = slice(sub * SUB, (sub + 1) * SUB)
                got = gather(csend[step, pl.ds(g, 1), at])
                for c in range(3):
                    buf[c : c + 1, at] = got[c]
            for b in range(quota // LANES):
                live = lane < fill[:, b : b + 1]
                buf[3:4, b * LANES : (b + 1) * LANES] = jnp.where(live, 1.0, 0.0)

        @pl.loop(0, groups - 1)
        def _(k):
            to = mod(i + 1 + k)
            send_gather(to, sbuf.at[step, to])
            pair_copy(step, k).start()

        send_gather(i, rbuf.at[step, i])

        @pl.loop(0, groups)
        def _(g):
            for sub in range(quota // SUB):
                at = slice(sub * SUB, (sub + 1) * SUB)
                got = gather(crecv[step, pl.ds(g, 1), at], g, sub)
                for c in range(3):
                    local[g, c : c + 1, at] = got[c]

        if step == 0:
            set_scale(coef)
            for c in range(fields):
                xh[c * nodes : (c + 1) * nodes, :] = along_nodes(fwd[...], state[c])
        else:
            for copy in coef_copies:
                copy.wait()
            arrived = jnp.where(
                lax.broadcasted_iota(jnp.int32, (8, cross), 1) < half,
                coef_in[0], coef_in[1],
            )
            arrived = jnp.concatenate([arrived, arrived], axis=0)
            moved = sum(dot_nt(p, cross_hot[0]) for p in split3(arrived))
            set_scale(coef * keeps[0] + moved[:1])

        acc[...] = jnp.zeros_like(acc)

        def scatter(g):
            delta = rbuf[step, g, 0:3] - local[g, 0:3]
            radius = jnp.sum(delta * delta, axis=0, keepdims=True)
            live = rbuf[step, g, 3:4] > 0.5
            force = jnp.where(live, 0.5 * delta / (1.0 + radius), 0.0)
            node = lax.div(crecv[step, pl.ds(g, 1), :], fdev).astype(F32)
            wide = jnp.concatenate([iota[:nodes]] * (quota // LANES), axis=1)
            node_hot = jnp.where(wide == tall(node, nodes), BF16(1), BF16(0))
            high, low = split(force)
            spread = [
                node_hot * tall(p[c : c + 1].astype(F32), nodes)
                for p in (high, low)
                for c in range(3)
            ]
            acc[...] += dot_nt(jnp.concatenate(spread, axis=0), hot[g])

        scatter(i)

        @pl.loop(0, groups - 1)
        def _(k):
            source = mod(i + groups - 1 - k)
            pair_arrival(step, source).wait_recv()
            scatter(source)

        for c in range(fields):
            at = slice(c * nodes, (c + 1) * nodes)
            block = xh[at, :]
            if c < 3:
                low_at = slice(npos + c * nodes, npos + (c + 1) * nodes)
                block += along_nodes(fwd[...], acc[at, :] + acc[low_at, :])
            xh[at, :] = block * scale[...]

        table = cross_hot[step]
        high, low = split(xh[...])
        picked = dot(high, table) + dot(low, table)
        top, bottom = picked[: rows // 2], picked[rows // 2 :]
        first = lax.broadcasted_iota(jnp.int32, (rows // 2, cross), 1) < half
        mout[step, 0] = jnp.where(first, top, pltpu.roll(bottom, half, 1))
        mout[step, 1] = jnp.where(first, pltpu.roll(top, half, 1), bottom)
        copies = [
            pltpu.make_async_remote_copy(
                src_ref=mout.at[step, d], dst_ref=min_.at[step, d],
                send_sem=m_send.at[step, d], recv_sem=m_recv.at[step, d],
                device_id=dev, device_id_type=MESH,
            )
            for d, dev in enumerate((down_dev, up_dev))
        ]
        for copy in copies:
            copy.start()
        for copy in copies:
            copy.wait()
        above, below = min_[step, 0], min_[step, 1]
        came = jnp.concatenate(
            [
                jnp.where(first, above, pltpu.roll(below, half, 1)),
                jnp.where(first, pltpu.roll(above, half, 1), below),
            ],
            axis=0,
        )
        high, low = split(came)
        xh[...] = xh[...] * keeps[step] + dot_nt(high, table) + dot_nt(low, table)

        if step < STEPS - 1:
            for c in range(3):
                block = xh[c * nodes : (c + 1) * nodes, :]
                set_parts(c, along_nodes(inv[...], block))
        else:
            for c in range(fields):
                block = xh[c * nodes : (c + 1) * nodes, :]
                out[c] = along_nodes(inv[...], block)

    for step in range(STEPS):

        @pl.loop(0, groups - 1)
        def _(k):
            pair_copy(step, k).wait_send()


def per_device(groups, n_stream, state, stiffness, crossing, csend, crecv, cfill):
    fields, nodes, fdev = state.shape
    quota = csend.shape[2]
    cross = crossing.shape[1]
    rows = fields * nodes
    fwd, inv, lam = cosine_tables(nodes)
    iota = np.repeat(np.arange(HALF_SLOTS)[:, None], LANES, axis=1)
    iota = iota.astype(ml_dtypes.bfloat16)
    vmem = pl.BlockSpec(memory_space=pltpu.VMEM)
    return pl.pallas_call(
        functools.partial(kernel, groups, n_stream),
        out_shape=jax.ShapeDtypeStruct(state.shape, F32),
        in_specs=[vmem] * 10,
        out_specs=vmem,
        scratch_shapes=[
            pltpu.VMEM((rows, fdev), F32),
            pltpu.VMEM((6 * nodes, fdev), BF16),
            pltpu.VMEM((groups, fdev, quota), BF16),
            pltpu.VMEM((groups, 4, quota), F32),
            pltpu.VMEM((6 * nodes, fdev), F32),
            pltpu.VMEM((nodes, fdev), F32),
            pltpu.VMEM((2, 8, cross), F32),
            pltpu.VMEM((8, cross), F32),
            pltpu.VMEM((STEPS, groups, 4, quota), F32),
            pltpu.VMEM((STEPS, groups, 4, quota), F32),
            pltpu.VMEM((STEPS, 2, rows // 2, cross), F32),
            pltpu.VMEM((STEPS, 2, rows // 2, cross), F32),
            pltpu.SemaphoreType.DMA((2,)),
            pltpu.SemaphoreType.DMA((2,)),
            pltpu.SemaphoreType.DMA((STEPS, groups)),
            pltpu.SemaphoreType.DMA((STEPS, groups)),
            pltpu.SemaphoreType.DMA((STEPS, 2)),
            pltpu.SemaphoreType.DMA((STEPS, 2)),
        ],
        compiler_params=pltpu.CompilerParams(
            collective_id=0, has_side_effects=True, vmem_limit_bytes=48 * 2**20
        ),
    )(
        state, stiffness.reshape(1, fdev), crossing, csend, crecv, cfill,
        jnp.asarray(fwd), jnp.asarray(inv), jnp.asarray(lam), jnp.asarray(iota),
    )


def solution(mesh):
    cells = ("span", "stream")
    placed = (
        P(None, None, cells),
        P(cells),
        P(None, cells),
        P(None, None, cells),
        P(None, None, cells),
        P(None, None, cells),
    )
    return jax.shard_map(
        functools.partial(per_device, mesh.shape["span"], mesh.shape["stream"]),
        mesh=mesh,
        in_specs=placed,
        out_specs=P(None, None, cells),
        check_vma=False,
    )
```

```python
import functools
import math

import jax
import jax.numpy as jnp
import ml_dtypes
import numpy as np
from jax import lax
from jax.experimental import pallas as pl
from jax.experimental.pallas import tpu as pltpu
from jax.sharding import PartitionSpec as P

STEPS = 2
MESH = pl.DeviceIdType.MESH
F32 = jnp.float32
BF16 = jnp.bfloat16
LANES = 128
HALF_SLOTS = 256
SUB = 256


def cosine_tables(nodes):
    k = np.arange(nodes)[:, None]
    n = np.arange(nodes)[None, :]
    basis = np.sqrt(2.0 / nodes) * np.cos(np.pi * (n + 0.5) * k / nodes)
    basis[0] /= math.sqrt(2.0)

    def stacked(matrix):
        high = matrix.astype(ml_dtypes.bfloat16)
        low = (matrix - high.astype(np.float64)).astype(ml_dtypes.bfloat16)
        return np.concatenate([high, high, low, np.zeros_like(low)], axis=1)

    lam = 2.0 - 2.0 * np.cos(np.pi * np.arange(nodes) / nodes)
    lam = np.repeat(lam[:, None], LANES, axis=1).astype(np.float32)
    return stacked(basis), stacked(basis.T), lam


def split(x):
    high = x.astype(BF16)
    return high, (x - high.astype(F32)).astype(BF16)


def split3(x):
    high, rest = x.astype(BF16), None
    rest = x - high.astype(F32)
    mid = rest.astype(BF16)
    return high, mid, (rest - mid.astype(F32)).astype(BF16)


def dot(a, b):
    return jnp.dot(a, b, preferred_element_type=F32)


def dot_nt(a, b):
    return lax.dot_general(a, b, (((1,), (1,)), ((), ())), preferred_element_type=F32)


def along_nodes(matrix, block):
    high, low = split(block)
    return dot(matrix, jnp.concatenate([high, low, high], axis=0))


def tall(row, rows):
    tile = jnp.broadcast_to(row, (16, row.shape[1])).astype(BF16)
    return jnp.concatenate([tile] * (rows // 16), axis=0)


def kernel(
    groups, n_stream,
    state_hbm, coef_hbm, crossing_hbm, csend_hbm, crecv_hbm, cfill_hbm, mats_hbm, lam_hbm,
    out,
    state, coef0, crossing, csend, crecv, cfill, mats, lam, iota,
    xh, parts, hot, local, acc, scale, base, coef_in, coef_out, sbuf, rbuf, mout, min_,
    l_sem, c_send, c_recv, p_send, p_recv, m_send, m_recv,
):
    fields, nodes, fdev = state.shape
    quota = csend.shape[2]
    cross = crossing.shape[1]
    half = cross // 2
    npos = 3 * nodes
    i = lax.axis_index("span")
    j = lax.axis_index("stream")
    down_dev = (i, lax.rem(j + 1, n_stream))
    up_dev = (i, lax.rem(j + n_stream - 1, n_stream))
    pos_at, rot_at = slice(0, npos), slice(npos, 2 * npos)

    def mod(v):
        return lax.rem(v, groups)

    barrier = pltpu.get_barrier_semaphore()
    for dev in (down_dev, up_dev):
        pl.semaphore_signal(barrier, inc=1, device_id=dev, device_id_type=MESH)
    for k in range(1, groups):
        pl.semaphore_signal(
            barrier, inc=1, device_id=(mod(i + k), j), device_id_type=MESH
        )

    moves = [
        (state_hbm.at[0:3], state.at[0:3]),
        (csend_hbm, csend),
        (cfill_hbm, cfill),
        (crecv_hbm, crecv),
        (crossing_hbm, crossing),
        (coef_hbm, coef0),
        (mats_hbm, mats),
        (lam_hbm, lam),
        (state_hbm.at[3:6], state.at[3:6]),
    ]
    loads = [
        pltpu.make_async_copy(src, dst, l_sem.at[n])
        for n, (src, dst) in enumerate(moves)
    ]
    for copy in loads:
        copy.start()

    iota[...] = (
        lax.broadcasted_iota(jnp.int32, (HALF_SLOTS, LANES), 0).astype(F32).astype(BF16)
    )
    lane = lax.broadcasted_iota(jnp.int32, (1, LANES), 1)
    node_iota = lax.broadcasted_iota(jnp.int32, (nodes, SUB), 0)

    def slot_hot(slot, q):
        pieces = []
        for part in range(fdev // HALF_SLOTS):
            rel = slot - part * HALF_SLOTS
            inside = (rel >= 0) & (rel < HALF_SLOTS)
            val = jnp.where(inside, rel, -1).astype(F32)
            wide = jnp.concatenate([iota[...]] * (q // LANES), axis=1)
            same = wide == tall(val, HALF_SLOTS)
            pieces.append(jnp.where(same, BF16(1), BF16(0)))
        return jnp.concatenate(pieces, axis=0)

    def gather(index, keep_at=None, sub=0):
        slot = lax.rem(index, fdev)
        node = lax.div(index, fdev)
        table = slot_hot(slot, SUB)
        if keep_at is not None:
            hot[keep_at, :, sub * SUB : (sub + 1) * SUB] = table
        picked = dot(parts[...], table)
        picked = picked[:npos] + picked[npos:]
        mask = node_iota == node
        return [
            jnp.sum(
                jnp.where(mask, picked[c * nodes : (c + 1) * nodes], 0.0),
                axis=0, keepdims=True,
            )
            for c in range(3)
        ]

    def set_parts(block):
        high, low = split(block)
        parts[:npos, :] = high
        parts[npos:, :] = low

    def forward(block):
        return along_nodes(mats[:nodes, : 3 * nodes].astype(BF16), block)

    def backward(block):
        back = mats[nodes:, : 3 * nodes].astype(BF16)
        return jnp.concatenate(
            [along_nodes(back, block[c * nodes : (c + 1) * nodes]) for c in range(3)],
            axis=0,
        )

    def set_scale(c):
        for b in range(fdev // LANES):
            at = slice(b * LANES, (b + 1) * LANES)
            scale[:, at] = 1.0 / (1.0 + lam[...] * c[:, at])

    def pair_copy(step, k):
        to = mod(i + 1 + k)
        return pltpu.make_async_remote_copy(
            src_ref=sbuf.at[step, to], dst_ref=rbuf.at[step, i],
            send_sem=p_send.at[step, to], recv_sem=p_recv.at[step, i],
            device_id=(to, j), device_id_type=MESH,
        )

    def pair_arrival(step, source):
        return pltpu.make_async_remote_copy(
            src_ref=sbuf.at[step, source], dst_ref=rbuf.at[step, source],
            send_sem=p_send.at[step, source], recv_sem=p_recv.at[step, source],
            device_id=(source, j), device_id_type=MESH,
        )

    first = lax.broadcasted_iota(jnp.int32, (npos // 2, cross), 1) < half

    def fibre_copies(step, h):
        return [
            pltpu.make_async_remote_copy(
                src_ref=mout.at[step, h, d], dst_ref=min_.at[step, h, d],
                send_sem=m_send.at[step, h, d], recv_sem=m_recv.at[step, h, d],
                device_id=dev, device_id_type=MESH,
            )
            for d, dev in enumerate((down_dev, up_dev))
        ]

    def leave(step, h, block, table):
        high, low = split(block)
        picked = dot(high, table) + dot(low, table)
        top, bottom = picked[: npos // 2], picked[npos // 2 :]
        mout[step, h, 0] = jnp.where(first, top, pltpu.roll(bottom, half, 1))
        mout[step, h, 1] = jnp.where(first, pltpu.roll(top, half, 1), bottom)
        for copy in fibre_copies(step, h):
            copy.start()

    def arrive(step, h):
        for copy in fibre_copies(step, h):
            copy.wait()
        above, below = min_[step, h, 0], min_[step, h, 1]
        return jnp.concatenate(
            [
                jnp.where(first, above, pltpu.roll(below, half, 1)),
                jnp.where(first, pltpu.roll(above, half, 1), below),
            ],
            axis=0,
        )

    def inserted(came, table):
        high, low = split(came)
        return dot_nt(high, table) + dot_nt(low, table)

    def send_gather(step, g, buf):
        fill = cfill[step, pl.ds(g, 1), :]
        for sub in range(quota // SUB):
            at = slice(sub * SUB, (sub + 1) * SUB)
            got = gather(csend[step, pl.ds(g, 1), at])
            for c in range(3):
                buf[c : c + 1, at] = got[c]
        for b in range(quota // LANES):
            live = lane < fill[:, b : b + 1]
            buf[3:4, b * LANES : (b + 1) * LANES] = jnp.where(live, 1.0, 0.0)

    for copy in loads[:3]:
        copy.wait()
    set_parts(jnp.concatenate([state[c] for c in range(3)], axis=0))

    for step in range(STEPS):
        send_gather(step, i, rbuf.at[step, i])
        if step == 0:
            pl.semaphore_wait(barrier, groups + 1)

        @pl.loop(0, groups - 1)
        def _(k):
            to = mod(i + 1 + k)
            send_gather(step, to, sbuf.at[step, to])
            pair_copy(step, k).start()

        if step == 0:
            for copy in loads[3:]:
                copy.wait()
            cross_hot = [slot_hot(crossing[s : s + 1, :], cross) for s in range(STEPS)]
            ones = jnp.ones((16, cross), BF16)
            keeps = [1.0 - dot_nt(ones, t)[:1] for t in cross_hot]
            coef = coef0[...]
            wide_coef = jnp.broadcast_to(coef, (16, fdev))
            leaving = sum(dot(p, cross_hot[0]) for p in split3(wide_coef))
            coef_out[...] = leaving[:8]
            coef_copies = [
                pltpu.make_async_remote_copy(
                    src_ref=coef_out, dst_ref=coef_in.at[d],
                    send_sem=c_send.at[d], recv_sem=c_recv.at[d],
                    device_id=dev, device_id_type=MESH,
                )
                for d, dev in enumerate((down_dev, up_dev))
            ]
            for copy in coef_copies:
                copy.start()
            set_scale(coef)
            for c in range(3, fields):
                xh[c * nodes : (c + 1) * nodes, :] = forward(state[c]) * scale[...]
            leave(step, 1, xh[rot_at, :], cross_hot[step])

        @pl.loop(0, groups)
        def _(g):
            for sub in range(quota // SUB):
                at = slice(sub * SUB, (sub + 1) * SUB)
                got = gather(crecv[step, pl.ds(g, 1), at], g, sub)
                for c in range(3):
                    local[g, c : c + 1, at] = got[c]

        if step == 0:
            for c in range(3):
                xh[c * nodes : (c + 1) * nodes, :] = forward(state[c])
        else:
            for copy in coef_copies:
                copy.wait()
            arrived = jnp.where(
                lax.broadcasted_iota(jnp.int32, (8, cross), 1) < half,
                coef_in[0], coef_in[1],
            )
            arrived = jnp.concatenate([arrived, arrived], axis=0)
            moved = sum(dot_nt(p, cross_hot[0]) for p in split3(arrived))
            set_scale(coef * keeps[0] + moved[:1])
            xh[pos_at, :] = xh[pos_at, :] * keeps[0] + inserted(came, cross_hot[0])
            turned = inserted(arrive(0, 1), cross_hot[0])
            for c in range(3):
                at = slice(npos + c * nodes, npos + (c + 1) * nodes)
                moved_in = turned[c * nodes : (c + 1) * nodes]
                xh[at, :] = (xh[at, :] * keeps[0] + moved_in) * scale[...]
            leave(step, 1, xh[rot_at, :], cross_hot[step])

        acc[...] = jnp.zeros_like(acc)

        def scatter(g):
            delta = rbuf[step, g, 0:3] - local[g, 0:3]
            radius = jnp.sum(delta * delta, axis=0, keepdims=True)
            live = rbuf[step, g, 3:4] > 0.5
            force = jnp.where(live, 0.5 * delta / (1.0 + radius), 0.0)
            node = lax.div(crecv[step, pl.ds(g, 1), :], fdev).astype(F32)
            wide = jnp.concatenate([iota[:nodes]] * (quota // LANES), axis=1)
            node_hot = jnp.where(wide == tall(node, nodes), BF16(1), BF16(0))
            high, low = split(force)
            spread = [
                node_hot * tall(p[c : c + 1].astype(F32), nodes)
                for p in (high, low)
                for c in range(3)
            ]
            acc[...] += dot_nt(jnp.concatenate(spread, axis=0), hot[g])

        scatter(i)

        @pl.loop(0, groups - 1)
        def _(k):
            source = mod(i + groups - 1 - k)
            pair_arrival(step, source).wait_recv()
            scatter(source)

        for c in range(3):
            at = slice(c * nodes, (c + 1) * nodes)
            low_at = slice(npos + c * nodes, npos + (c + 1) * nodes)
            push = forward(acc[at, :] + acc[low_at, :])
            xh[at, :] = (xh[at, :] + push) * scale[...]
        table, keep = cross_hot[step], keeps[step]
        leave(step, 0, xh[pos_at, :], table)

        base[...] = backward(xh[pos_at, :] * keep)
        if step < STEPS - 1:
            came = arrive(step, 0)
            set_parts(base[...] + inserted(backward(came), table))
        else:
            turned = backward(xh[rot_at, :] * keep)
            turned += inserted(backward(arrive(step, 1)), table)
            for c in range(3):
                out[3 + c] = turned[c * nodes : (c + 1) * nodes]
            placed = base[...] + inserted(backward(arrive(step, 0)), table)
            for c in range(3):
                out[c] = placed[c * nodes : (c + 1) * nodes]

    for step in range(STEPS):

        @pl.loop(0, groups - 1)
        def _(k):
            pair_copy(step, k).wait_send()


def per_device(groups, n_stream, state, stiffness, crossing, csend, crecv, cfill):
    fields, nodes, fdev = state.shape
    quota = csend.shape[2]
    cross = crossing.shape[1]
    rows = fields * nodes
    fwd, inv, lam = cosine_tables(nodes)
    mats = np.concatenate([fwd, inv], axis=0).astype(np.float32)
    hbm = pl.BlockSpec(memory_space=pltpu.HBM)
    return pl.pallas_call(
        functools.partial(kernel, groups, n_stream),
        out_shape=jax.ShapeDtypeStruct(state.shape, F32),
        in_specs=[hbm] * 8,
        out_specs=pl.BlockSpec(memory_space=pltpu.VMEM),
        scratch_shapes=[
            pltpu.VMEM(state.shape, F32),
            pltpu.VMEM((1, fdev), F32),
            pltpu.VMEM(crossing.shape, jnp.int32),
            pltpu.VMEM(csend.shape, jnp.int32),
            pltpu.VMEM(crecv.shape, jnp.int32),
            pltpu.VMEM(cfill.shape, jnp.int32),
            pltpu.VMEM(mats.shape, F32),
            pltpu.VMEM(lam.shape, F32),
            pltpu.VMEM((HALF_SLOTS, LANES), BF16),
            pltpu.VMEM((rows, fdev), F32),
            pltpu.VMEM((6 * nodes, fdev), BF16),
            pltpu.VMEM((groups, fdev, quota), BF16),
            pltpu.VMEM((groups, 4, quota), F32),
            pltpu.VMEM((6 * nodes, fdev), F32),
            pltpu.VMEM((nodes, fdev), F32),
            pltpu.VMEM((3 * nodes, fdev), F32),
            pltpu.VMEM((2, 8, cross), F32),
            pltpu.VMEM((8, cross), F32),
            pltpu.VMEM((STEPS, groups, 4, quota), F32),
            pltpu.VMEM((STEPS, groups, 4, quota), F32),
            pltpu.VMEM((STEPS, 2, 2, rows // 4, cross), F32),
            pltpu.VMEM((STEPS, 2, 2, rows // 4, cross), F32),
            pltpu.SemaphoreType.DMA((9,)),
            pltpu.SemaphoreType.DMA((2,)),
            pltpu.SemaphoreType.DMA((2,)),
            pltpu.SemaphoreType.DMA((STEPS, groups)),
            pltpu.SemaphoreType.DMA((STEPS, groups)),
            pltpu.SemaphoreType.DMA((STEPS, 2, 2)),
            pltpu.SemaphoreType.DMA((STEPS, 2, 2)),
        ],
        compiler_params=pltpu.CompilerParams(
            collective_id=0, has_side_effects=True, vmem_limit_bytes=63 * 2**20
        ),
    )(
        state, stiffness.reshape(1, fdev), crossing, csend, crecv, cfill,
        jnp.asarray(mats), jnp.asarray(lam),
    )


def solution(mesh):
    cells = ("span", "stream")
    placed = (
        P(None, None, cells),
        P(cells),
        P(None, cells),
        P(None, None, cells),
        P(None, None, cells),
        P(None, None, cells),
    )
    return jax.shard_map(
        functools.partial(per_device, mesh.shape["span"], mesh.shape["stream"]),
        mesh=mesh,
        in_specs=placed,
        out_specs=P(None, None, cells),
        check_vma=False,
    )
```

```python
import functools
import math

import jax
import jax.numpy as jnp
import ml_dtypes
import numpy as np
from jax import lax
from jax.experimental import pallas as pl
from jax.experimental.pallas import tpu as pltpu
from jax.sharding import PartitionSpec as P

STEPS = 2
MESH = pl.DeviceIdType.MESH
F32 = jnp.float32
BF16 = jnp.bfloat16
LANES = 128
HALF_SLOTS = 256
SUB = 256


def cosine_tables(nodes):
    k = np.arange(nodes)[:, None]
    n = np.arange(nodes)[None, :]
    basis = np.sqrt(2.0 / nodes) * np.cos(np.pi * (n + 0.5) * k / nodes)
    basis[0] /= math.sqrt(2.0)

    def stacked(matrix):
        high = matrix.astype(ml_dtypes.bfloat16)
        low = (matrix - high.astype(np.float64)).astype(ml_dtypes.bfloat16)
        return np.concatenate([high, high, low, np.zeros_like(low)], axis=1)

    lam = 2.0 - 2.0 * np.cos(np.pi * np.arange(nodes) / nodes)
    lam = np.repeat(lam[:, None], LANES, axis=1).astype(np.float32)
    return stacked(basis), stacked(basis.T), lam


def split(x):
    high = x.astype(BF16)
    return high, (x - high.astype(F32)).astype(BF16)


def split3(x):
    high, rest = x.astype(BF16), None
    rest = x - high.astype(F32)
    mid = rest.astype(BF16)
    return high, mid, (rest - mid.astype(F32)).astype(BF16)


def dot(a, b):
    return jnp.dot(a, b, preferred_element_type=F32)


def dot_nt(a, b):
    return lax.dot_general(a, b, (((1,), (1,)), ((), ())), preferred_element_type=F32)


def along_nodes(matrix, block):
    high, low = split(block)
    return dot(matrix, jnp.concatenate([high, low, high], axis=0))


def tall(row, rows):
    tile = jnp.broadcast_to(row, (16, row.shape[1])).astype(BF16)
    return jnp.concatenate([tile] * (rows // 16), axis=0)


def kernel(
    groups, n_stream,
    state_hbm, coef_hbm, crossing_hbm, csend_hbm, crecv_hbm, cfill_hbm, mats_hbm, lam_hbm,
    out,
    state, coef0, crossing, csend, crecv, cfill, mats, lam, iota,
    xh, parts, hot, local, acc, scale, base, ahead, cross_col, moving, coef_in, coef_out, sbuf, rbuf, mout, min_,
    l_sem, c_send, c_recv, p_send, p_recv, m_send, m_recv,
):
    fields, nodes, fdev = state.shape
    quota = csend.shape[2]
    cross = crossing.shape[1]
    half = cross // 2
    npos = 3 * nodes
    i = lax.axis_index("span")
    j = lax.axis_index("stream")
    down_dev = (i, lax.rem(j + 1, n_stream))
    up_dev = (i, lax.rem(j + n_stream - 1, n_stream))
    pos_at, rot_at = slice(0, npos), slice(npos, 2 * npos)

    def mod(v):
        return lax.rem(v, groups)

    barrier = pltpu.get_barrier_semaphore()
    for dev in (down_dev, up_dev):
        pl.semaphore_signal(barrier, inc=1, device_id=dev, device_id_type=MESH)
    for k in range(1, groups):
        pl.semaphore_signal(
            barrier, inc=1, device_id=(mod(i + k), j), device_id_type=MESH
        )

    moves = [
        (state_hbm.at[0:3], state.at[0:3]),
        (csend_hbm, csend),
        (cfill_hbm, cfill),
        (crecv_hbm, crecv),
        (crossing_hbm, crossing),
        (coef_hbm, coef0),
        (mats_hbm, mats),
        (lam_hbm, lam),
        (state_hbm.at[3:6], state.at[3:6]),
    ]
    loads = [
        pltpu.make_async_copy(src, dst, l_sem.at[n])
        for n, (src, dst) in enumerate(moves)
    ]
    for copy in loads:
        copy.start()

    iota[...] = (
        lax.broadcasted_iota(jnp.int32, (HALF_SLOTS, LANES), 0).astype(F32).astype(BF16)
    )
    lane = lax.broadcasted_iota(jnp.int32, (1, LANES), 1)
    node_iota = lax.broadcasted_iota(jnp.int32, (nodes, SUB), 0)

    def slot_hot(slot, q):
        pieces = []
        for part in range(fdev // HALF_SLOTS):
            rel = slot - part * HALF_SLOTS
            inside = (rel >= 0) & (rel < HALF_SLOTS)
            val = jnp.where(inside, rel, -1).astype(F32)
            wide = jnp.concatenate([iota[...]] * (q // LANES), axis=1)
            same = wide == tall(val, HALF_SLOTS)
            pieces.append(jnp.where(same, BF16(1), BF16(0)))
        return jnp.concatenate(pieces, axis=0)

    def locate(index):
        if fdev & (fdev - 1) == 0:
            return index & (fdev - 1), index >> (fdev.bit_length() - 1)
        return lax.rem(index, fdev), lax.div(index, fdev)

    def gather(index, keep_at=None, sub=0):
        slot, node = locate(index)
        table = slot_hot(slot, SUB)
        if keep_at is not None:
            hot[keep_at, :, sub * SUB : (sub + 1) * SUB] = table
        picked = dot(parts[...], table)
        return at_nodes(picked[:npos] + picked[npos:], node)

    def at_nodes(picked, node):
        mask = node_iota == node
        return [
            jnp.sum(
                jnp.where(mask, picked[c * nodes : (c + 1) * nodes], 0.0),
                axis=0, keepdims=True,
            )
            for c in range(3)
        ]

    def set_parts(block):
        high, low = split(block)
        parts[:npos, :] = high
        parts[npos:, :] = low

    def forward(block):
        return along_nodes(mats[:nodes, : 3 * nodes].astype(BF16), block)

    def backward(block):
        back = mats[nodes:, : 3 * nodes].astype(BF16)
        return jnp.concatenate(
            [along_nodes(back, block[c * nodes : (c + 1) * nodes]) for c in range(3)],
            axis=0,
        )

    def set_scale(c):
        for b in range(fdev // LANES):
            at = slice(b * LANES, (b + 1) * LANES)
            scale[:, at] = 1.0 / (1.0 + lam[...] * c[:, at])

    def pair_copy(step, k):
        to = mod(i + 1 + k)
        return pltpu.make_async_remote_copy(
            src_ref=sbuf.at[step, to], dst_ref=rbuf.at[step, i],
            send_sem=p_send.at[step, to], recv_sem=p_recv.at[step, i],
            device_id=(to, j), device_id_type=MESH,
        )

    def pair_arrival(step, source):
        return pltpu.make_async_remote_copy(
            src_ref=sbuf.at[step, source], dst_ref=rbuf.at[step, source],
            send_sem=p_send.at[step, source], recv_sem=p_recv.at[step, source],
            device_id=(source, j), device_id_type=MESH,
        )

    first = lax.broadcasted_iota(jnp.int32, (npos // 2, cross), 1) < half

    def fibre_copies(step, h):
        return [
            pltpu.make_async_remote_copy(
                src_ref=mout.at[step, h, d], dst_ref=min_.at[step, h, d],
                send_sem=m_send.at[step, h, d], recv_sem=m_recv.at[step, h, d],
                device_id=dev, device_id_type=MESH,
            )
            for d, dev in enumerate((down_dev, up_dev))
        ]

    def leave(step, h, block, table):
        high, low = split(block)
        picked = dot(high, table) + dot(low, table)
        top, bottom = picked[: npos // 2], picked[npos // 2 :]
        mout[step, h, 0] = jnp.where(first, top, pltpu.roll(bottom, half, 1))
        mout[step, h, 1] = jnp.where(first, pltpu.roll(top, half, 1), bottom)
        for copy in fibre_copies(step, h):
            copy.start()

    def arrive(step, h):
        for copy in fibre_copies(step, h):
            copy.wait()
        above, below = min_[step, h, 0], min_[step, h, 1]
        return jnp.concatenate(
            [
                jnp.where(first, above, pltpu.roll(below, half, 1)),
                jnp.where(first, pltpu.roll(above, half, 1), below),
            ],
            axis=0,
        )

    def inserted(came, table):
        high, low = split(came)
        return dot_nt(high, table) + dot_nt(low, table)

    def send_gather(step, g, buf):
        fill = cfill[step, pl.ds(g, 1), :]
        for sub in range(quota // SUB):
            at = slice(sub * SUB, (sub + 1) * SUB)
            got = gather(csend[step, pl.ds(g, 1), at])
            for c in range(3):
                buf[c : c + 1, at] = got[c]
        for b in range(quota // LANES):
            live = lane < fill[:, b : b + 1]
            buf[3:4, b * LANES : (b + 1) * LANES] = jnp.where(live, 1.0, 0.0)

    def arrived_gather(step, g, moving, buf):
        for sub in range(quota // SUB):
            at = slice(sub * SUB, (sub + 1) * SUB)
            slot, node = locate(csend[step, pl.ds(g, 1), at])
            wide = jnp.concatenate([cross_col[...]] * (SUB // LANES), axis=1)
            table = jnp.where(wide == slot, 1.0, 0.0).astype(BF16)
            got = at_nodes(dot(moving, jnp.concatenate([table, table], axis=0)), node)
            for c in range(3):
                buf[c : c + 1, at] = ahead[g, c : c + 1, at] + got[c]
        buf[3:4, :] = ahead[g, 3:4, :]

    for copy in loads[:3]:
        copy.wait()
    set_parts(jnp.concatenate([state[c] for c in range(3)], axis=0))

    for step in range(STEPS):
        if step == 0:
            send_gather(step, i, rbuf.at[step, i])
            pl.semaphore_wait(barrier, groups + 1)

            @pl.loop(0, groups - 1)
            def _(k):
                to = mod(i + 1 + k)
                send_gather(step, to, sbuf.at[step, to])
                pair_copy(step, k).start()

        else:

            @pl.loop(0, groups - 1)
            def _(k):
                to = mod(i + 1 + k)
                arrived_gather(step, to, moving[...], sbuf.at[step, to])
                pair_copy(step, k).start()

            arrived_gather(step, i, moving[...], rbuf.at[step, i])
            set_parts(base[...] + inserted(came_nodes, cross_hot[step - 1]))

        if step == 0:
            for copy in loads[3:]:
                copy.wait()
            cross_hot = [slot_hot(crossing[s : s + 1, :], cross) for s in range(STEPS)]
            ones = jnp.ones((16, cross), BF16)
            keeps = [1.0 - dot_nt(ones, t)[:1] for t in cross_hot]
            coef = coef0[...]
            wide_coef = jnp.broadcast_to(coef, (16, fdev))
            leaving = sum(dot(p, cross_hot[0]) for p in split3(wide_coef))
            coef_out[...] = leaving[:8]
            coef_copies = [
                pltpu.make_async_remote_copy(
                    src_ref=coef_out, dst_ref=coef_in.at[d],
                    send_sem=c_send.at[d], recv_sem=c_recv.at[d],
                    device_id=dev, device_id_type=MESH,
                )
                for d, dev in enumerate((down_dev, up_dev))
            ]
            for copy in coef_copies:
                copy.start()
            set_scale(coef)
            for c in range(3, fields):
                xh[c * nodes : (c + 1) * nodes, :] = forward(state[c]) * scale[...]
            leave(step, 1, xh[rot_at, :], cross_hot[step])

        @pl.loop(0, groups)
        def _(g):
            for sub in range(quota // SUB):
                at = slice(sub * SUB, (sub + 1) * SUB)
                got = gather(crecv[step, pl.ds(g, 1), at], g, sub)
                for c in range(3):
                    local[g, c : c + 1, at] = got[c]

        if step == 0:
            for c in range(3):
                xh[c * nodes : (c + 1) * nodes, :] = forward(state[c])
        else:
            for copy in coef_copies:
                copy.wait()
            arrived = jnp.where(
                lax.broadcasted_iota(jnp.int32, (8, cross), 1) < half,
                coef_in[0], coef_in[1],
            )
            arrived = jnp.concatenate([arrived, arrived], axis=0)
            moved = sum(dot_nt(p, cross_hot[0]) for p in split3(arrived))
            set_scale(coef * keeps[0] + moved[:1])
            xh[pos_at, :] = xh[pos_at, :] * keeps[0] + inserted(came, cross_hot[0])
            turned = inserted(arrive(0, 1), cross_hot[0])
            for c in range(3):
                at = slice(npos + c * nodes, npos + (c + 1) * nodes)
                moved_in = turned[c * nodes : (c + 1) * nodes]
                xh[at, :] = (xh[at, :] * keeps[0] + moved_in) * scale[...]
            leave(step, 1, xh[rot_at, :], cross_hot[step])

        acc[...] = jnp.zeros_like(acc)

        def scatter(g):
            delta = rbuf[step, g, 0:3] - local[g, 0:3]
            radius = jnp.sum(delta * delta, axis=0, keepdims=True)
            live = rbuf[step, g, 3:4] > 0.5
            force = jnp.where(live, 0.5 * delta / (1.0 + radius), 0.0)
            node = locate(crecv[step, pl.ds(g, 1), :])[1].astype(F32)
            wide = jnp.concatenate([iota[:nodes]] * (quota // LANES), axis=1)
            node_hot = jnp.where(wide == tall(node, nodes), BF16(1), BF16(0))
            high, low = split(force)
            spread = [
                node_hot * tall(p[c : c + 1].astype(F32), nodes)
                for p in (high, low)
                for c in range(3)
            ]
            acc[...] += dot_nt(jnp.concatenate(spread, axis=0), hot[g])

        scatter(i)

        @pl.loop(0, groups - 1)
        def _(k):
            source = mod(i + groups - 1 - k)
            pair_arrival(step, source).wait_recv()
            scatter(source)

        for c in range(3):
            at = slice(c * nodes, (c + 1) * nodes)
            low_at = slice(npos + c * nodes, npos + (c + 1) * nodes)
            push = forward(acc[at, :] + acc[low_at, :])
            xh[at, :] = (xh[at, :] + push) * scale[...]
        table, keep = cross_hot[step], keeps[step]
        leave(step, 0, xh[pos_at, :], table)

        base[...] = backward(xh[pos_at, :] * keep)
        if step < STEPS - 1:
            set_parts(base[...])
            column = jnp.broadcast_to(crossing[step : step + 1, :].astype(F32), (LANES, cross))
            cross_col[...] = column.T.astype(jnp.int32)

            @pl.loop(0, groups)
            def _(g):
                send_gather(step + 1, g, ahead.at[g])

            came = arrive(step, 0)
            came_nodes = backward(came)
            moving[...] = jnp.concatenate(split(came_nodes), axis=1)
        else:
            turned = backward(xh[rot_at, :] * keep)
            turned += inserted(backward(arrive(step, 1)), table)
            for c in range(3):
                out[3 + c] = turned[c * nodes : (c + 1) * nodes]
            placed = base[...] + inserted(backward(arrive(step, 0)), table)
            for c in range(3):
                out[c] = placed[c * nodes : (c + 1) * nodes]

    for step in range(STEPS):

        @pl.loop(0, groups - 1)
        def _(k):
            pair_copy(step, k).wait_send()


def per_device(groups, n_stream, state, stiffness, crossing, csend, crecv, cfill):
    fields, nodes, fdev = state.shape
    quota = csend.shape[2]
    cross = crossing.shape[1]
    rows = fields * nodes
    fwd, inv, lam = cosine_tables(nodes)
    mats = np.concatenate([fwd, inv], axis=0).astype(np.float32)
    hbm = pl.BlockSpec(memory_space=pltpu.HBM)
    return pl.pallas_call(
        functools.partial(kernel, groups, n_stream),
        out_shape=pltpu.VMEM(state.shape, F32),
        in_specs=[hbm] * 8,
        out_specs=pl.BlockSpec(memory_space=pltpu.VMEM),
        scratch_shapes=[
            pltpu.VMEM(state.shape, F32),
            pltpu.VMEM((1, fdev), F32),
            pltpu.VMEM(crossing.shape, jnp.int32),
            pltpu.VMEM(csend.shape, jnp.int32),
            pltpu.VMEM(crecv.shape, jnp.int32),
            pltpu.VMEM(cfill.shape, jnp.int32),
            pltpu.VMEM(mats.shape, F32),
            pltpu.VMEM(lam.shape, F32),
            pltpu.VMEM((HALF_SLOTS, LANES), BF16),
            pltpu.VMEM((rows, fdev), F32),
            pltpu.VMEM((6 * nodes, fdev), BF16),
            pltpu.VMEM((groups, fdev, quota), BF16),
            pltpu.VMEM((groups, 4, quota), F32),
            pltpu.VMEM((6 * nodes, fdev), F32),
            pltpu.VMEM((nodes, fdev), F32),
            pltpu.VMEM((3 * nodes, fdev), F32),
            pltpu.VMEM((groups, 4, quota), F32),
            pltpu.VMEM((cross, LANES), jnp.int32),
            pltpu.VMEM((3 * nodes, 2 * cross), BF16),
            pltpu.VMEM((2, 8, cross), F32),
            pltpu.VMEM((8, cross), F32),
            pltpu.VMEM((STEPS, groups, 4, quota), F32),
            pltpu.VMEM((STEPS, groups, 4, quota), F32),
            pltpu.VMEM((STEPS, 2, 2, rows // 4, cross), F32),
            pltpu.VMEM((STEPS, 2, 2, rows // 4, cross), F32),
            pltpu.SemaphoreType.DMA((9,)),
            pltpu.SemaphoreType.DMA((2,)),
            pltpu.SemaphoreType.DMA((2,)),
            pltpu.SemaphoreType.DMA((STEPS, groups)),
            pltpu.SemaphoreType.DMA((STEPS, groups)),
            pltpu.SemaphoreType.DMA((STEPS, 2, 2)),
            pltpu.SemaphoreType.DMA((STEPS, 2, 2)),
        ],
        compiler_params=pltpu.CompilerParams(
            collective_id=0, has_side_effects=True, vmem_limit_bytes=40 * 2**20
        ),
    )(
        *(
            pltpu.with_memory_space_constraint(x, pltpu.HBM)
            for x in (
                state, stiffness.reshape(1, fdev), crossing, csend, crecv, cfill,
                jnp.asarray(mats), jnp.asarray(lam),
            )
        )
    )


def solution(mesh):
    cells = ("span", "stream")
    placed = (
        P(None, None, cells),
        P(cells),
        P(None, cells),
        P(None, None, cells),
        P(None, None, cells),
        P(None, None, cells),
    )
    return jax.shard_map(
        functools.partial(per_device, mesh.shape["span"], mesh.shape["stream"]),
        mesh=mesh,
        in_specs=placed,
        out_specs=P(None, None, cells),
        check_vma=False,
    )
```

```python
import functools
import math

import jax
import jax.numpy as jnp
import ml_dtypes
import numpy as np
from jax import lax
from jax.experimental import pallas as pl
from jax.experimental.pallas import tpu as pltpu
from jax.sharding import PartitionSpec as P

STEPS = 2
MESH = pl.DeviceIdType.MESH
F32 = jnp.float32
BF16 = jnp.bfloat16
LANES = 128
HALF_SLOTS = 256
SUB = 512


def cosine_tables(nodes):
    k = np.arange(nodes)[:, None]
    n = np.arange(nodes)[None, :]
    basis = np.sqrt(2.0 / nodes) * np.cos(np.pi * (n + 0.5) * k / nodes)
    basis[0] /= math.sqrt(2.0)

    def stacked(matrix):
        high = matrix.astype(ml_dtypes.bfloat16)
        low = (matrix - high.astype(np.float64)).astype(ml_dtypes.bfloat16)
        return np.concatenate([high, high, low, np.zeros_like(low)], axis=1)

    lam = 2.0 - 2.0 * np.cos(np.pi * np.arange(nodes) / nodes)
    lam = np.repeat(lam[:, None], LANES, axis=1).astype(np.float32)
    return stacked(basis), stacked(basis.T), lam


def split(x):
    high = x.astype(BF16)
    return high, (x - high.astype(F32)).astype(BF16)


def split3(x):
    high, rest = x.astype(BF16), None
    rest = x - high.astype(F32)
    mid = rest.astype(BF16)
    return high, mid, (rest - mid.astype(F32)).astype(BF16)


def dot(a, b):
    return jnp.dot(a, b, preferred_element_type=F32)


def dot_nt(a, b):
    return lax.dot_general(a, b, (((1,), (1,)), ((), ())), preferred_element_type=F32)


def along_nodes(matrix, block):
    high, low = split(block)
    return dot(matrix, jnp.concatenate([high, low, high], axis=0))


def tall(row, rows):
    tile = jnp.broadcast_to(row, (16, row.shape[1])).astype(BF16)
    return jnp.concatenate([tile] * (rows // 16), axis=0)


def kernel(
    groups, n_stream,
    state_hbm, coef_hbm, crossing_hbm, csend_hbm, crecv_hbm, cfill_hbm, mats_hbm, lam_hbm,
    out,
    state, coef0, crossing, csend, crecv, cfill, mats, lam, iota,
    xh, parts, hot, local, acc, scale, base, ahead, cross_col, moving, coef_in, coef_out, sbuf, rbuf, mout, min_,
    l_sem, c_send, c_recv, p_send, p_recv, m_send, m_recv,
):
    fields, nodes, fdev = state.shape
    quota = csend.shape[2]
    cross = crossing.shape[1]
    half = cross // 2
    npos = 3 * nodes
    i = lax.axis_index("span")
    j = lax.axis_index("stream")
    down_dev = (i, lax.rem(j + 1, n_stream))
    up_dev = (i, lax.rem(j + n_stream - 1, n_stream))
    pos_at, rot_at = slice(0, npos), slice(npos, 2 * npos)

    def mod(v):
        return lax.rem(v, groups)

    barrier = pltpu.get_barrier_semaphore()
    for dev in (down_dev, up_dev):
        pl.semaphore_signal(barrier, inc=1, device_id=dev, device_id_type=MESH)
    for k in range(1, groups):
        pl.semaphore_signal(
            barrier, inc=1, device_id=(mod(i + k), j), device_id_type=MESH
        )

    moves = [
        (state_hbm.at[0:3], state.at[0:3]),
        (csend_hbm, csend),
        (cfill_hbm, cfill),
        (crecv_hbm, crecv),
        (crossing_hbm, crossing),
        (coef_hbm, coef0),
        (mats_hbm, mats),
        (lam_hbm, lam),
        (state_hbm.at[3:6], state.at[3:6]),
    ]
    loads = [
        pltpu.make_async_copy(src, dst, l_sem.at[n])
        for n, (src, dst) in enumerate(moves)
    ]
    for copy in loads:
        copy.start()

    iota[...] = (
        lax.broadcasted_iota(jnp.int32, (HALF_SLOTS, LANES), 0).astype(F32).astype(BF16)
    )
    lane = lax.broadcasted_iota(jnp.int32, (1, LANES), 1)
    node_iota = lax.broadcasted_iota(jnp.int32, (nodes, SUB), 0)

    def slot_hot(slot, q):
        pieces = []
        for part in range(fdev // HALF_SLOTS):
            rel = slot - part * HALF_SLOTS
            inside = (rel >= 0) & (rel < HALF_SLOTS)
            val = jnp.where(inside, rel, -1).astype(F32)
            wide = jnp.concatenate([iota[...]] * (q // LANES), axis=1)
            same = wide == tall(val, HALF_SLOTS)
            pieces.append(jnp.where(same, BF16(1), BF16(0)))
        return jnp.concatenate(pieces, axis=0)

    def locate(index):
        if fdev & (fdev - 1) == 0:
            return index & (fdev - 1), index >> (fdev.bit_length() - 1)
        return lax.rem(index, fdev), lax.div(index, fdev)

    def gather(index, keep_at=None, sub=0):
        slot, node = locate(index)
        table = slot_hot(slot, SUB)
        if keep_at is not None:
            hot[keep_at, :, sub * SUB : (sub + 1) * SUB] = table
        picked = dot(parts[...], table)
        return at_nodes(picked[:npos] + picked[npos:], node)

    def at_nodes(picked, node):
        mask = node_iota == node
        return [
            jnp.sum(
                jnp.where(mask, picked[c * nodes : (c + 1) * nodes], 0.0),
                axis=0, keepdims=True,
            )
            for c in range(3)
        ]

    def set_parts(block):
        high, low = split(block)
        parts[:npos, :] = high
        parts[npos:, :] = low

    def forward(block):
        return along_nodes(mats[:nodes, : 3 * nodes].astype(BF16), block)

    def backward(block):
        back = mats[nodes:, : 3 * nodes].astype(BF16)
        return jnp.concatenate(
            [along_nodes(back, block[c * nodes : (c + 1) * nodes]) for c in range(3)],
            axis=0,
        )

    def set_scale(c):
        for b in range(fdev // LANES):
            at = slice(b * LANES, (b + 1) * LANES)
            scale[:, at] = 1.0 / (1.0 + lam[...] * c[:, at])

    def pair_copy(step, k):
        to = mod(i + 1 + k)
        return pltpu.make_async_remote_copy(
            src_ref=sbuf.at[step, to], dst_ref=rbuf.at[step, i],
            send_sem=p_send.at[step, to], recv_sem=p_recv.at[step, i],
            device_id=(to, j), device_id_type=MESH,
        )

    def pair_arrival(step, source):
        return pltpu.make_async_remote_copy(
            src_ref=sbuf.at[step, source], dst_ref=rbuf.at[step, source],
            send_sem=p_send.at[step, source], recv_sem=p_recv.at[step, source],
            device_id=(source, j), device_id_type=MESH,
        )

    first = lax.broadcasted_iota(jnp.int32, (npos // 2, cross), 1) < half

    def fibre_copies(step, h):
        return [
            pltpu.make_async_remote_copy(
                src_ref=mout.at[step, h, d], dst_ref=min_.at[step, h, d],
                send_sem=m_send.at[step, h, d], recv_sem=m_recv.at[step, h, d],
                device_id=dev, device_id_type=MESH,
            )
            for d, dev in enumerate((down_dev, up_dev))
        ]

    def leave(step, h, block, table):
        high, low = split(block)
        picked = dot(high, table) + dot(low, table)
        top, bottom = picked[: npos // 2], picked[npos // 2 :]
        mout[step, h, 0] = jnp.where(first, top, pltpu.roll(bottom, half, 1))
        mout[step, h, 1] = jnp.where(first, pltpu.roll(top, half, 1), bottom)
        for copy in fibre_copies(step, h):
            copy.start()

    def arrive(step, h):
        for copy in fibre_copies(step, h):
            copy.wait()
        above, below = min_[step, h, 0], min_[step, h, 1]
        return jnp.concatenate(
            [
                jnp.where(first, above, pltpu.roll(below, half, 1)),
                jnp.where(first, pltpu.roll(above, half, 1), below),
            ],
            axis=0,
        )

    def inserted(came, table):
        high, low = split(came)
        return dot_nt(high, table) + dot_nt(low, table)

    def send_gather(step, g, buf):
        fill = cfill[step, pl.ds(g, 1), :]
        for sub in range(quota // SUB):
            at = slice(sub * SUB, (sub + 1) * SUB)
            got = gather(csend[step, pl.ds(g, 1), at])
            for c in range(3):
                buf[c : c + 1, at] = got[c]
        for b in range(quota // LANES):
            live = lane < fill[:, b : b + 1]
            buf[3:4, b * LANES : (b + 1) * LANES] = jnp.where(live, 1.0, 0.0)

    def arrived_gather(step, g, moving, buf):
        for sub in range(quota // SUB):
            at = slice(sub * SUB, (sub + 1) * SUB)
            slot, node = locate(csend[step, pl.ds(g, 1), at])
            wide = jnp.concatenate([cross_col[...]] * (SUB // LANES), axis=1)
            table = jnp.where(wide == slot, 1.0, 0.0).astype(BF16)
            got = at_nodes(dot(moving, jnp.concatenate([table, table], axis=0)), node)
            for c in range(3):
                buf[c : c + 1, at] = ahead[g, c : c + 1, at] + got[c]
        buf[3:4, :] = ahead[g, 3:4, :]

    for copy in loads[:3]:
        copy.wait()
    set_parts(jnp.concatenate([state[c] for c in range(3)], axis=0))

    for step in range(STEPS):
        if step == 0:
            send_gather(step, i, rbuf.at[step, i])
            pl.semaphore_wait(barrier, groups + 1)

            @pl.loop(0, groups - 1)
            def _(k):
                to = mod(i + 1 + k)
                send_gather(step, to, sbuf.at[step, to])
                pair_copy(step, k).start()

        else:

            @pl.loop(0, groups - 1)
            def _(k):
                to = mod(i + 1 + k)
                arrived_gather(step, to, moving[...], sbuf.at[step, to])
                pair_copy(step, k).start()

            arrived_gather(step, i, moving[...], rbuf.at[step, i])
            set_parts(base[...] + inserted(came_nodes, cross_hot[step - 1]))

        if step == 0:
            for copy in loads[3:]:
                copy.wait()
            cross_hot = [slot_hot(crossing[s : s + 1, :], cross) for s in range(STEPS)]
            ones = jnp.ones((16, cross), BF16)
            keeps = [1.0 - dot_nt(ones, t)[:1] for t in cross_hot]
            coef = coef0[...]
            wide_coef = jnp.broadcast_to(coef, (16, fdev))
            leaving = sum(dot(p, cross_hot[0]) for p in split3(wide_coef))
            coef_out[...] = leaving[:8]
            coef_copies = [
                pltpu.make_async_remote_copy(
                    src_ref=coef_out, dst_ref=coef_in.at[d],
                    send_sem=c_send.at[d], recv_sem=c_recv.at[d],
                    device_id=dev, device_id_type=MESH,
                )
                for d, dev in enumerate((down_dev, up_dev))
            ]
            for copy in coef_copies:
                copy.start()
            set_scale(coef)
            for c in range(3, fields):
                xh[c * nodes : (c + 1) * nodes, :] = forward(state[c]) * scale[...]
            leave(step, 1, xh[rot_at, :], cross_hot[step])

        @pl.loop(0, groups)
        def _(g):
            for sub in range(quota // SUB):
                at = slice(sub * SUB, (sub + 1) * SUB)
                got = gather(crecv[step, pl.ds(g, 1), at], g, sub)
                for c in range(3):
                    local[g, c : c + 1, at] = got[c]

        if step == 0:
            for c in range(3):
                xh[c * nodes : (c + 1) * nodes, :] = forward(state[c])
        else:
            for copy in coef_copies:
                copy.wait()
            arrived = jnp.where(
                lax.broadcasted_iota(jnp.int32, (8, cross), 1) < half,
                coef_in[0], coef_in[1],
            )
            arrived = jnp.concatenate([arrived, arrived], axis=0)
            moved = sum(dot_nt(p, cross_hot[0]) for p in split3(arrived))
            set_scale(coef * keeps[0] + moved[:1])
            xh[pos_at, :] = xh[pos_at, :] * keeps[0] + inserted(came, cross_hot[0])
            turned = inserted(arrive(0, 1), cross_hot[0])
            for c in range(3):
                at = slice(npos + c * nodes, npos + (c + 1) * nodes)
                moved_in = turned[c * nodes : (c + 1) * nodes]
                xh[at, :] = (xh[at, :] * keeps[0] + moved_in) * scale[...]
            leave(step, 1, xh[rot_at, :], cross_hot[step])

        acc[...] = jnp.zeros_like(acc)

        def scatter(g):
            delta = rbuf[step, g, 0:3] - local[g, 0:3]
            radius = jnp.sum(delta * delta, axis=0, keepdims=True)
            live = rbuf[step, g, 3:4] > 0.5
            force = jnp.where(live, 0.5 * delta / (1.0 + radius), 0.0)
            node = locate(crecv[step, pl.ds(g, 1), :])[1].astype(F32)
            wide = jnp.concatenate([iota[:nodes]] * (quota // LANES), axis=1)
            node_hot = jnp.where(wide == tall(node, nodes), BF16(1), BF16(0))
            high, low = split(force)
            spread = [
                node_hot * tall(p[c : c + 1].astype(F32), nodes)
                for p in (high, low)
                for c in range(3)
            ]
            acc[...] += dot_nt(jnp.concatenate(spread, axis=0), hot[g])

        scatter(i)

        @pl.loop(0, groups - 1)
        def _(k):
            source = mod(i + groups - 1 - k)
            pair_arrival(step, source).wait_recv()
            scatter(source)

        for c in range(3):
            at = slice(c * nodes, (c + 1) * nodes)
            low_at = slice(npos + c * nodes, npos + (c + 1) * nodes)
            push = forward(acc[at, :] + acc[low_at, :])
            xh[at, :] = (xh[at, :] + push) * scale[...]
        table, keep = cross_hot[step], keeps[step]
        leave(step, 0, xh[pos_at, :], table)

        base[...] = backward(xh[pos_at, :] * keep)
        if step < STEPS - 1:
            set_parts(base[...])
            column = jnp.broadcast_to(crossing[step : step + 1, :].astype(F32), (LANES, cross))
            cross_col[...] = column.T.astype(jnp.int32)

            @pl.loop(0, groups)
            def _(g):
                send_gather(step + 1, g, ahead.at[g])

            came = arrive(step, 0)
            came_nodes = backward(came)
            moving[...] = jnp.concatenate(split(came_nodes), axis=1)
        else:
            turned = backward(xh[rot_at, :] * keep)
            turned += inserted(backward(arrive(step, 1)), table)
            for c in range(3):
                out[3 + c] = turned[c * nodes : (c + 1) * nodes]
            placed = base[...] + inserted(backward(arrive(step, 0)), table)
            for c in range(3):
                out[c] = placed[c * nodes : (c + 1) * nodes]

    for step in range(STEPS):

        @pl.loop(0, groups - 1)
        def _(k):
            pair_copy(step, k).wait_send()


def per_device(groups, n_stream, state, stiffness, crossing, csend, crecv, cfill):
    fields, nodes, fdev = state.shape
    quota = csend.shape[2]
    cross = crossing.shape[1]
    rows = fields * nodes
    fwd, inv, lam = cosine_tables(nodes)
    mats = np.concatenate([fwd, inv], axis=0).astype(np.float32)
    hbm = pl.BlockSpec(memory_space=pltpu.HBM)
    return pl.pallas_call(
        functools.partial(kernel, groups, n_stream),
        out_shape=pltpu.VMEM(state.shape, F32),
        in_specs=[hbm] * 8,
        out_specs=pl.BlockSpec(memory_space=pltpu.VMEM),
        scratch_shapes=[
            pltpu.VMEM(state.shape, F32),
            pltpu.VMEM((1, fdev), F32),
            pltpu.VMEM(crossing.shape, jnp.int32),
            pltpu.VMEM(csend.shape, jnp.int32),
            pltpu.VMEM(crecv.shape, jnp.int32),
            pltpu.VMEM(cfill.shape, jnp.int32),
            pltpu.VMEM(mats.shape, F32),
            pltpu.VMEM(lam.shape, F32),
            pltpu.VMEM((HALF_SLOTS, LANES), BF16),
            pltpu.VMEM((rows, fdev), F32),
            pltpu.VMEM((6 * nodes, fdev), BF16),
            pltpu.VMEM((groups, fdev, quota), BF16),
            pltpu.VMEM((groups, 4, quota), F32),
            pltpu.VMEM((6 * nodes, fdev), F32),
            pltpu.VMEM((nodes, fdev), F32),
            pltpu.VMEM((3 * nodes, fdev), F32),
            pltpu.VMEM((groups, 4, quota), F32),
            pltpu.VMEM((cross, LANES), jnp.int32),
            pltpu.VMEM((3 * nodes, 2 * cross), BF16),
            pltpu.VMEM((2, 8, cross), F32),
            pltpu.VMEM((8, cross), F32),
            pltpu.VMEM((STEPS, groups, 4, quota), F32),
            pltpu.VMEM((STEPS, groups, 4, quota), F32),
            pltpu.VMEM((STEPS, 2, 2, rows // 4, cross), F32),
            pltpu.VMEM((STEPS, 2, 2, rows // 4, cross), F32),
            pltpu.SemaphoreType.DMA((9,)),
            pltpu.SemaphoreType.DMA((2,)),
            pltpu.SemaphoreType.DMA((2,)),
            pltpu.SemaphoreType.DMA((STEPS, groups)),
            pltpu.SemaphoreType.DMA((STEPS, groups)),
            pltpu.SemaphoreType.DMA((STEPS, 2, 2)),
            pltpu.SemaphoreType.DMA((STEPS, 2, 2)),
        ],
        compiler_params=pltpu.CompilerParams(
            collective_id=0, has_side_effects=True, vmem_limit_bytes=40 * 2**20
        ),
    )(
        *(
            pltpu.with_memory_space_constraint(x, pltpu.HBM)
            for x in (
                state, stiffness.reshape(1, fdev), crossing, csend, crecv, cfill,
                jnp.asarray(mats), jnp.asarray(lam),
            )
        )
    )


def solution(mesh):
    cells = ("span", "stream")
    placed = (
        P(None, None, cells),
        P(cells),
        P(None, cells),
        P(None, None, cells),
        P(None, None, cells),
        P(None, None, cells),
    )
    return jax.shard_map(
        functools.partial(per_device, mesh.shape["span"], mesh.shape["stream"]),
        mesh=mesh,
        in_specs=placed,
        out_specs=P(None, None, cells),
        check_vma=False,
    )
```

```python
import functools
import math

import jax
import jax.numpy as jnp
import ml_dtypes
import numpy as np
from jax import lax
from jax.experimental import pallas as pl
from jax.experimental.pallas import tpu as pltpu
from jax.sharding import PartitionSpec as P

STEPS = 2
MESH = pl.DeviceIdType.MESH
F32 = jnp.float32
BF16 = jnp.bfloat16
LANES = 128
HALF_SLOTS = 256
SUB = 256
BY_LANES = 2


def cosine_tables(nodes):
    k = np.arange(nodes)[:, None]
    n = np.arange(nodes)[None, :]
    basis = np.sqrt(2.0 / nodes) * np.cos(np.pi * (n + 0.5) * k / nodes)
    basis[0] /= math.sqrt(2.0)

    def stacked(matrix):
        high = matrix.astype(ml_dtypes.bfloat16)
        low = (matrix - high.astype(np.float64)).astype(ml_dtypes.bfloat16)
        return np.concatenate([high, high, low, np.zeros_like(low)], axis=1)

    lam = 2.0 - 2.0 * np.cos(np.pi * np.arange(nodes) / nodes)
    lam = np.repeat(lam[:, None], LANES, axis=1).astype(np.float32)
    return stacked(basis), stacked(basis.T), lam


def split(x):
    high = x.astype(BF16)
    return high, (x - high.astype(F32)).astype(BF16)


def split3(x):
    high, rest = x.astype(BF16), None
    rest = x - high.astype(F32)
    mid = rest.astype(BF16)
    return high, mid, (rest - mid.astype(F32)).astype(BF16)


def dot(a, b):
    return jnp.dot(a, b, preferred_element_type=F32)


def dot_nt(a, b):
    return lax.dot_general(a, b, (((1,), (1,)), ((), ())), preferred_element_type=F32)


def along_nodes(matrix, block):
    high, low = split(block)
    return dot(matrix, jnp.concatenate([high, low, high], axis=0))


def tall(row, rows):
    tile = jnp.broadcast_to(row, (16, row.shape[1])).astype(BF16)
    return jnp.concatenate([tile] * (rows // 16), axis=0)


def kernel(
    groups, n_stream,
    state_hbm, coef_hbm, crossing_hbm, csend_hbm, crecv_hbm, cfill_hbm, mats_hbm, lam_hbm,
    out,
    state, coef0, crossing, csend, crecv, cfill, mats, lam, iota,
    xh, parts, exact, hot, local, acc, scale, base, ahead, cross_col, moving, coef_in, coef_out, sbuf, rbuf, mout, min_,
    l_sem, c_send, c_recv, p_send, p_recv, m_send, m_recv,
):
    fields, nodes, fdev = state.shape
    quota = csend.shape[2]
    cross = crossing.shape[1]
    half = cross // 2
    npos = 3 * nodes
    i = lax.axis_index("span")
    j = lax.axis_index("stream")
    down_dev = (i, lax.rem(j + 1, n_stream))
    up_dev = (i, lax.rem(j + n_stream - 1, n_stream))
    pos_at, rot_at = slice(0, npos), slice(npos, 2 * npos)

    def mod(v):
        return lax.rem(v, groups)

    barrier = pltpu.get_barrier_semaphore()
    for dev in (down_dev, up_dev):
        pl.semaphore_signal(barrier, inc=1, device_id=dev, device_id_type=MESH)
    for k in range(1, groups):
        pl.semaphore_signal(
            barrier, inc=1, device_id=(mod(i + k), j), device_id_type=MESH
        )

    moves = [
        (state_hbm.at[0:3], state.at[0:3]),
        (csend_hbm, csend),
        (cfill_hbm, cfill),
        (crecv_hbm, crecv),
        (crossing_hbm, crossing),
        (coef_hbm, coef0),
        (mats_hbm, mats),
        (lam_hbm, lam),
        (state_hbm.at[3:6], state.at[3:6]),
    ]
    loads = [
        pltpu.make_async_copy(src, dst, l_sem.at[n])
        for n, (src, dst) in enumerate(moves)
    ]
    for copy in loads:
        copy.start()

    iota[...] = (
        lax.broadcasted_iota(jnp.int32, (HALF_SLOTS, LANES), 0).astype(F32).astype(BF16)
    )
    lane = lax.broadcasted_iota(jnp.int32, (1, LANES), 1)
    node_iota = lax.broadcasted_iota(jnp.int32, (nodes, SUB), 0)

    def slot_hot(slot, q):
        pieces = []
        for part in range(fdev // HALF_SLOTS):
            rel = slot - part * HALF_SLOTS
            inside = (rel >= 0) & (rel < HALF_SLOTS)
            val = jnp.where(inside, rel, -1).astype(F32)
            wide = jnp.concatenate([iota[...]] * (q // LANES), axis=1)
            same = wide == tall(val, HALF_SLOTS)
            pieces.append(jnp.where(same, BF16(1), BF16(0)))
        return jnp.concatenate(pieces, axis=0)

    def locate(index):
        if fdev & (fdev - 1) == 0:
            return index & (fdev - 1), index >> (fdev.bit_length() - 1)
        return lax.rem(index, fdev), lax.div(index, fdev)

    def gather(index, keep_at=None, sub=0):
        slot, node = locate(index)
        table = slot_hot(slot, SUB)
        if keep_at is not None:
            hot[keep_at, :, sub * SUB : (sub + 1) * SUB] = table
        picked = dot(parts[...], table)
        return at_nodes(picked[:npos] + picked[npos:], node)

    def lane_gather(index):
        slot, node = locate(index)
        at_lane = jnp.broadcast_to(slot & (LANES - 1), (npos, LANES))
        block = jnp.broadcast_to(slot >> 7, (npos, LANES))
        picked = jnp.zeros((npos, LANES), F32)
        for b in range(fdev // LANES):
            part = jnp.take_along_axis(
                exact[:, b * LANES : (b + 1) * LANES], at_lane, axis=1,
                mode="promise_in_bounds",
            )
            picked = jnp.where(block == b, part, picked)
        return at_nodes(picked, node)

    def gather_group(indices, step, g, buf, keep_at=None):
        subs = quota // SUB
        for sub in range(subs):
            at = slice(sub * SUB, (sub + 1) * SUB)
            index = indices[step, pl.ds(g, 1), at]
            if sub < subs - BY_LANES:
                got = gather(index, keep_at, sub)
                for c in range(3):
                    buf[c : c + 1, at] = got[c]
                continue
            if keep_at is not None:
                hot[keep_at, :, at] = slot_hot(locate(index)[0], SUB)
            for n in range(SUB // LANES):
                piece = slice(n * LANES, (n + 1) * LANES)
                to = slice(sub * SUB + n * LANES, sub * SUB + (n + 1) * LANES)
                got = lane_gather(index[:, piece])
                for c in range(3):
                    buf[c : c + 1, to] = got[c]

    def at_nodes(picked, node):
        mask = node_iota[:, : node.shape[1]] == node
        return [
            jnp.sum(
                jnp.where(mask, picked[c * nodes : (c + 1) * nodes], 0.0),
                axis=0, keepdims=True,
            )
            for c in range(3)
        ]

    def set_parts(block):
        high, low = split(block)
        parts[:npos, :] = high
        parts[npos:, :] = low
        exact[...] = block

    def forward(block):
        return along_nodes(mats[:nodes, : 3 * nodes].astype(BF16), block)

    def backward(block):
        back = mats[nodes:, : 3 * nodes].astype(BF16)
        return jnp.concatenate(
            [along_nodes(back, block[c * nodes : (c + 1) * nodes]) for c in range(3)],
            axis=0,
        )

    def set_scale(c):
        for b in range(fdev // LANES):
            at = slice(b * LANES, (b + 1) * LANES)
            scale[:, at] = 1.0 / (1.0 + lam[...] * c[:, at])

    def pair_copy(step, k):
        to = mod(i + 1 + k)
        return pltpu.make_async_remote_copy(
            src_ref=sbuf.at[step, to], dst_ref=rbuf.at[step, i],
            send_sem=p_send.at[step, to], recv_sem=p_recv.at[step, i],
            device_id=(to, j), device_id_type=MESH,
        )

    def pair_arrival(step, source):
        return pltpu.make_async_remote_copy(
            src_ref=sbuf.at[step, source], dst_ref=rbuf.at[step, source],
            send_sem=p_send.at[step, source], recv_sem=p_recv.at[step, source],
            device_id=(source, j), device_id_type=MESH,
        )

    first = lax.broadcasted_iota(jnp.int32, (npos // 2, cross), 1) < half

    def fibre_copies(step, h):
        return [
            pltpu.make_async_remote_copy(
                src_ref=mout.at[step, h, d], dst_ref=min_.at[step, h, d],
                send_sem=m_send.at[step, h, d], recv_sem=m_recv.at[step, h, d],
                device_id=dev, device_id_type=MESH,
            )
            for d, dev in enumerate((down_dev, up_dev))
        ]

    def leave(step, h, block, table):
        high, low = split(block)
        picked = dot(high, table) + dot(low, table)
        top, bottom = picked[: npos // 2], picked[npos // 2 :]
        mout[step, h, 0] = jnp.where(first, top, pltpu.roll(bottom, half, 1))
        mout[step, h, 1] = jnp.where(first, pltpu.roll(top, half, 1), bottom)
        for copy in fibre_copies(step, h):
            copy.start()

    def arrive(step, h):
        for copy in fibre_copies(step, h):
            copy.wait()
        above, below = min_[step, h, 0], min_[step, h, 1]
        return jnp.concatenate(
            [
                jnp.where(first, above, pltpu.roll(below, half, 1)),
                jnp.where(first, pltpu.roll(above, half, 1), below),
            ],
            axis=0,
        )

    def inserted(came, table):
        high, low = split(came)
        return dot_nt(high, table) + dot_nt(low, table)

    def send_gather(step, g, buf):
        fill = cfill[step, pl.ds(g, 1), :]
        gather_group(csend, step, g, buf)
        for b in range(quota // LANES):
            live = lane < fill[:, b : b + 1]
            buf[3:4, b * LANES : (b + 1) * LANES] = jnp.where(live, 1.0, 0.0)

    def arrived_gather(step, g, moving, buf):
        for sub in range(quota // SUB):
            at = slice(sub * SUB, (sub + 1) * SUB)
            slot, node = locate(csend[step, pl.ds(g, 1), at])
            wide = jnp.concatenate([cross_col[...]] * (SUB // LANES), axis=1)
            table = jnp.where(wide == slot, 1.0, 0.0).astype(BF16)
            got = at_nodes(dot(moving, jnp.concatenate([table, table], axis=0)), node)
            for c in range(3):
                buf[c : c + 1, at] = ahead[g, c : c + 1, at] + got[c]
        buf[3:4, :] = ahead[g, 3:4, :]

    for copy in loads[:3]:
        copy.wait()
    set_parts(jnp.concatenate([state[c] for c in range(3)], axis=0))

    for step in range(STEPS):
        if step == 0:
            send_gather(step, i, rbuf.at[step, i])
            pl.semaphore_wait(barrier, groups + 1)

            @pl.loop(0, groups - 1)
            def _(k):
                to = mod(i + 1 + k)
                send_gather(step, to, sbuf.at[step, to])
                pair_copy(step, k).start()

        else:

            @pl.loop(0, groups - 1)
            def _(k):
                to = mod(i + 1 + k)
                arrived_gather(step, to, moving[...], sbuf.at[step, to])
                pair_copy(step, k).start()

            arrived_gather(step, i, moving[...], rbuf.at[step, i])
            set_parts(base[...] + inserted(came_nodes, cross_hot[step - 1]))

        if step == 0:
            for copy in loads[3:]:
                copy.wait()
            cross_hot = [slot_hot(crossing[s : s + 1, :], cross) for s in range(STEPS)]
            ones = jnp.ones((16, cross), BF16)
            keeps = [1.0 - dot_nt(ones, t)[:1] for t in cross_hot]
            coef = coef0[...]
            wide_coef = jnp.broadcast_to(coef, (16, fdev))
            leaving = sum(dot(p, cross_hot[0]) for p in split3(wide_coef))
            coef_out[...] = leaving[:8]
            coef_copies = [
                pltpu.make_async_remote_copy(
                    src_ref=coef_out, dst_ref=coef_in.at[d],
                    send_sem=c_send.at[d], recv_sem=c_recv.at[d],
                    device_id=dev, device_id_type=MESH,
                )
                for d, dev in enumerate((down_dev, up_dev))
            ]
            for copy in coef_copies:
                copy.start()
            set_scale(coef)
            for c in range(3, fields):
                xh[c * nodes : (c + 1) * nodes, :] = forward(state[c]) * scale[...]
            leave(step, 1, xh[rot_at, :], cross_hot[step])

        @pl.loop(0, groups)
        def _(g):
            gather_group(crecv, step, g, local.at[g], g)

        if step == 0:
            for c in range(3):
                xh[c * nodes : (c + 1) * nodes, :] = forward(state[c])
        else:
            for copy in coef_copies:
                copy.wait()
            arrived = jnp.where(
                lax.broadcasted_iota(jnp.int32, (8, cross), 1) < half,
                coef_in[0], coef_in[1],
            )
            arrived = jnp.concatenate([arrived, arrived], axis=0)
            moved = sum(dot_nt(p, cross_hot[0]) for p in split3(arrived))
            set_scale(coef * keeps[0] + moved[:1])
            xh[pos_at, :] = xh[pos_at, :] * keeps[0] + inserted(came, cross_hot[0])
            turned = inserted(arrive(0, 1), cross_hot[0])
            for c in range(3):
                at = slice(npos + c * nodes, npos + (c + 1) * nodes)
                moved_in = turned[c * nodes : (c + 1) * nodes]
                xh[at, :] = (xh[at, :] * keeps[0] + moved_in) * scale[...]
            leave(step, 1, xh[rot_at, :], cross_hot[step])

        acc[...] = jnp.zeros_like(acc)

        def scatter(g):
            delta = rbuf[step, g, 0:3] - local[g, 0:3]
            radius = jnp.sum(delta * delta, axis=0, keepdims=True)
            live = rbuf[step, g, 3:4] > 0.5
            force = jnp.where(live, 0.5 * delta / (1.0 + radius), 0.0)
            node = locate(crecv[step, pl.ds(g, 1), :])[1].astype(F32)
            wide = jnp.concatenate([iota[:nodes]] * (quota // LANES), axis=1)
            node_hot = jnp.where(wide == tall(node, nodes), BF16(1), BF16(0))
            high, low = split(force)
            spread = [
                node_hot * tall(p[c : c + 1].astype(F32), nodes)
                for p in (high, low)
                for c in range(3)
            ]
            acc[...] += dot_nt(jnp.concatenate(spread, axis=0), hot[g])

        scatter(i)

        @pl.loop(0, groups - 1)
        def _(k):
            source = mod(i + groups - 1 - k)
            pair_arrival(step, source).wait_recv()
            scatter(source)

        for c in range(3):
            at = slice(c * nodes, (c + 1) * nodes)
            low_at = slice(npos + c * nodes, npos + (c + 1) * nodes)
            push = forward(acc[at, :] + acc[low_at, :])
            xh[at, :] = (xh[at, :] + push) * scale[...]
        table, keep = cross_hot[step], keeps[step]
        leave(step, 0, xh[pos_at, :], table)

        base[...] = backward(xh[pos_at, :] * keep)
        if step < STEPS - 1:
            set_parts(base[...])
            column = jnp.broadcast_to(crossing[step : step + 1, :].astype(F32), (LANES, cross))
            cross_col[...] = column.T.astype(jnp.int32)

            @pl.loop(0, groups)
            def _(g):
                send_gather(step + 1, g, ahead.at[g])

            came = arrive(step, 0)
            came_nodes = backward(came)
            moving[...] = jnp.concatenate(split(came_nodes), axis=1)
        else:
            turned = backward(xh[rot_at, :] * keep)
            turned += inserted(backward(arrive(step, 1)), table)
            for c in range(3):
                out[3 + c] = turned[c * nodes : (c + 1) * nodes]
            placed = base[...] + inserted(backward(arrive(step, 0)), table)
            for c in range(3):
                out[c] = placed[c * nodes : (c + 1) * nodes]

    for step in range(STEPS):

        @pl.loop(0, groups - 1)
        def _(k):
            pair_copy(step, k).wait_send()


def per_device(groups, n_stream, state, stiffness, crossing, csend, crecv, cfill):
    fields, nodes, fdev = state.shape
    quota = csend.shape[2]
    cross = crossing.shape[1]
    rows = fields * nodes
    fwd, inv, lam = cosine_tables(nodes)
    mats = np.concatenate([fwd, inv], axis=0).astype(np.float32)
    hbm = pl.BlockSpec(memory_space=pltpu.HBM)
    return pl.pallas_call(
        functools.partial(kernel, groups, n_stream),
        out_shape=pltpu.VMEM(state.shape, F32),
        in_specs=[hbm] * 8,
        out_specs=pl.BlockSpec(memory_space=pltpu.VMEM),
        scratch_shapes=[
            pltpu.VMEM(state.shape, F32),
            pltpu.VMEM((1, fdev), F32),
            pltpu.VMEM(crossing.shape, jnp.int32),
            pltpu.VMEM(csend.shape, jnp.int32),
            pltpu.VMEM(crecv.shape, jnp.int32),
            pltpu.VMEM(cfill.shape, jnp.int32),
            pltpu.VMEM(mats.shape, F32),
            pltpu.VMEM(lam.shape, F32),
            pltpu.VMEM((HALF_SLOTS, LANES), BF16),
            pltpu.VMEM((rows, fdev), F32),
            pltpu.VMEM((6 * nodes, fdev), BF16),
            pltpu.VMEM((3 * nodes, fdev), F32),
            pltpu.VMEM((groups, fdev, quota), BF16),
            pltpu.VMEM((groups, 4, quota), F32),
            pltpu.VMEM((6 * nodes, fdev), F32),
            pltpu.VMEM((nodes, fdev), F32),
            pltpu.VMEM((3 * nodes, fdev), F32),
            pltpu.VMEM((groups, 4, quota), F32),
            pltpu.VMEM((cross, LANES), jnp.int32),
            pltpu.VMEM((3 * nodes, 2 * cross), BF16),
            pltpu.VMEM((2, 8, cross), F32),
            pltpu.VMEM((8, cross), F32),
            pltpu.VMEM((STEPS, groups, 4, quota), F32),
            pltpu.VMEM((STEPS, groups, 4, quota), F32),
            pltpu.VMEM((STEPS, 2, 2, rows // 4, cross), F32),
            pltpu.VMEM((STEPS, 2, 2, rows // 4, cross), F32),
            pltpu.SemaphoreType.DMA((9,)),
            pltpu.SemaphoreType.DMA((2,)),
            pltpu.SemaphoreType.DMA((2,)),
            pltpu.SemaphoreType.DMA((STEPS, groups)),
            pltpu.SemaphoreType.DMA((STEPS, groups)),
            pltpu.SemaphoreType.DMA((STEPS, 2, 2)),
            pltpu.SemaphoreType.DMA((STEPS, 2, 2)),
        ],
        compiler_params=pltpu.CompilerParams(
            collective_id=0, has_side_effects=True, vmem_limit_bytes=40 * 2**20
        ),
    )(
        *(
            pltpu.with_memory_space_constraint(x, pltpu.HBM)
            for x in (
                state, stiffness.reshape(1, fdev), crossing, csend, crecv, cfill,
                jnp.asarray(mats), jnp.asarray(lam),
            )
        )
    )


def solution(mesh):
    cells = ("span", "stream")
    placed = (
        P(None, None, cells),
        P(cells),
        P(None, cells),
        P(None, None, cells),
        P(None, None, cells),
        P(None, None, cells),
    )
    return jax.shard_map(
        functools.partial(per_device, mesh.shape["span"], mesh.shape["stream"]),
        mesh=mesh,
        in_specs=placed,
        out_specs=P(None, None, cells),
        check_vma=False,
    )
```

```python
import functools
import math

import jax
import jax.numpy as jnp
import ml_dtypes
import numpy as np
from jax import lax
from jax.experimental import pallas as pl
from jax.experimental.pallas import tpu as pltpu
from jax.sharding import PartitionSpec as P

STEPS = 2
MESH = pl.DeviceIdType.MESH
F32 = jnp.float32
BF16 = jnp.bfloat16
LANES = 128
HALF_SLOTS = 256
SUB = 256


def cosine_tables(nodes):
    k = np.arange(nodes)[:, None]
    n = np.arange(nodes)[None, :]
    basis = np.sqrt(2.0 / nodes) * np.cos(np.pi * (n + 0.5) * k / nodes)
    basis[0] /= math.sqrt(2.0)

    def stacked(matrix):
        high = matrix.astype(ml_dtypes.bfloat16)
        low = (matrix - high.astype(np.float64)).astype(ml_dtypes.bfloat16)
        return np.concatenate([high, high, low, np.zeros_like(low)], axis=1)

    lam = 2.0 - 2.0 * np.cos(np.pi * np.arange(nodes) / nodes)
    lam = np.repeat(lam[:, None], LANES, axis=1).astype(np.float32)
    return stacked(basis), stacked(basis.T), lam


def split(x):
    high = x.astype(BF16)
    return high, (x - high.astype(F32)).astype(BF16)


def split3(x):
    high, rest = x.astype(BF16), None
    rest = x - high.astype(F32)
    mid = rest.astype(BF16)
    return high, mid, (rest - mid.astype(F32)).astype(BF16)


def dot(a, b):
    return jnp.dot(a, b, preferred_element_type=F32)


def dot_nt(a, b):
    return lax.dot_general(a, b, (((1,), (1,)), ((), ())), preferred_element_type=F32)


def along_nodes(matrix, block):
    high, low = split(block)
    return dot(matrix, jnp.concatenate([high, low, high], axis=0))


def tall(row, rows):
    tile = jnp.broadcast_to(row, (16, row.shape[1])).astype(BF16)
    return jnp.concatenate([tile] * (rows // 16), axis=0)


def kernel(
    groups, n_stream,
    state_hbm, coef_hbm, crossing_hbm, csend_hbm, crecv_hbm, cfill_hbm, mats_hbm, lam_hbm,
    out,
    state, coef0, crossing, csend, crecv, cfill, mats, lam, iota,
    xh, parts, hot, local, acc, scale, base, ahead, cross_col, moving, hotx, spreads, lead, accx, coef_in, coef_out, sbuf, rbuf, mout, min_,
    l_sem, c_send, c_recv, p_send, p_recv, m_send, m_recv,
):
    fields, nodes, fdev = state.shape
    quota = csend.shape[2]
    cross = crossing.shape[1]
    half = cross // 2
    npos = 3 * nodes
    i = lax.axis_index("span")
    j = lax.axis_index("stream")
    down_dev = (i, lax.rem(j + 1, n_stream))
    up_dev = (i, lax.rem(j + n_stream - 1, n_stream))
    pos_at, rot_at = slice(0, npos), slice(npos, 2 * npos)

    def mod(v):
        return lax.rem(v, groups)

    barrier = pltpu.get_barrier_semaphore()
    for dev in (down_dev, up_dev):
        pl.semaphore_signal(barrier, inc=1, device_id=dev, device_id_type=MESH)
    for k in range(1, groups):
        pl.semaphore_signal(
            barrier, inc=1, device_id=(mod(i + k), j), device_id_type=MESH
        )

    moves = [
        (state_hbm.at[0:3], state.at[0:3]),
        (csend_hbm, csend),
        (cfill_hbm, cfill),
        (crecv_hbm, crecv),
        (crossing_hbm, crossing),
        (coef_hbm, coef0),
        (mats_hbm, mats),
        (lam_hbm, lam),
        (state_hbm.at[3:6], state.at[3:6]),
    ]
    loads = [
        pltpu.make_async_copy(src, dst, l_sem.at[n])
        for n, (src, dst) in enumerate(moves)
    ]
    for copy in loads:
        copy.start()

    iota[...] = (
        lax.broadcasted_iota(jnp.int32, (HALF_SLOTS, LANES), 0).astype(F32).astype(BF16)
    )
    lane = lax.broadcasted_iota(jnp.int32, (1, LANES), 1)
    node_iota = lax.broadcasted_iota(jnp.int32, (nodes, SUB), 0)

    def slot_hot(slot, q):
        pieces = []
        for part in range(fdev // HALF_SLOTS):
            rel = slot - part * HALF_SLOTS
            inside = (rel >= 0) & (rel < HALF_SLOTS)
            val = jnp.where(inside, rel, -1).astype(F32)
            wide = jnp.concatenate([iota[...]] * (q // LANES), axis=1)
            same = wide == tall(val, HALF_SLOTS)
            pieces.append(jnp.where(same, BF16(1), BF16(0)))
        return jnp.concatenate(pieces, axis=0)

    def locate(index):
        if fdev & (fdev - 1) == 0:
            return index & (fdev - 1), index >> (fdev.bit_length() - 1)
        return lax.rem(index, fdev), lax.div(index, fdev)

    def gather(index, keep_at=None, sub=0):
        slot, node = locate(index)
        table = slot_hot(slot, SUB)
        if keep_at is not None:
            hot[keep_at, :, sub * SUB : (sub + 1) * SUB] = table
        picked = dot(parts[...], table)
        return at_nodes(picked[:npos] + picked[npos:], node)

    def at_nodes(picked, node):
        mask = node_iota == node
        return [
            jnp.sum(
                jnp.where(mask, picked[c * nodes : (c + 1) * nodes], 0.0),
                axis=0, keepdims=True,
            )
            for c in range(3)
        ]

    def set_parts(block):
        high, low = split(block)
        parts[:npos, :] = high
        parts[npos:, :] = low

    def forward(block):
        return along_nodes(mats[:nodes, : 3 * nodes].astype(BF16), block)

    def backward(block):
        back = mats[nodes:, : 3 * nodes].astype(BF16)
        return jnp.concatenate(
            [along_nodes(back, block[c * nodes : (c + 1) * nodes]) for c in range(3)],
            axis=0,
        )

    def set_scale(c):
        for b in range(fdev // LANES):
            at = slice(b * LANES, (b + 1) * LANES)
            scale[:, at] = 1.0 / (1.0 + lam[...] * c[:, at])

    def pair_copy(step, k):
        to = mod(i + 1 + k)
        return pltpu.make_async_remote_copy(
            src_ref=sbuf.at[step, to], dst_ref=rbuf.at[step, i],
            send_sem=p_send.at[step, to], recv_sem=p_recv.at[step, i],
            device_id=(to, j), device_id_type=MESH,
        )

    def pair_arrival(step, source):
        return pltpu.make_async_remote_copy(
            src_ref=sbuf.at[step, source], dst_ref=rbuf.at[step, source],
            send_sem=p_send.at[step, source], recv_sem=p_recv.at[step, source],
            device_id=(source, j), device_id_type=MESH,
        )

    first = lax.broadcasted_iota(jnp.int32, (npos // 2, cross), 1) < half

    def fibre_copies(step, h):
        return [
            pltpu.make_async_remote_copy(
                src_ref=mout.at[step, h, d], dst_ref=min_.at[step, h, d],
                send_sem=m_send.at[step, h, d], recv_sem=m_recv.at[step, h, d],
                device_id=dev, device_id_type=MESH,
            )
            for d, dev in enumerate((down_dev, up_dev))
        ]

    def leave(step, h, block, table):
        send_off(step, h, pick(block, table))

    def pick(block, table):
        high, low = split(block)
        return dot(high, table) + dot(low, table)

    def send_off(step, h, picked):
        top, bottom = picked[: npos // 2], picked[npos // 2 :]
        mout[step, h, 0] = jnp.where(first, top, pltpu.roll(bottom, half, 1))
        mout[step, h, 1] = jnp.where(first, pltpu.roll(top, half, 1), bottom)
        for copy in fibre_copies(step, h):
            copy.start()

    def arrive(step, h):
        for copy in fibre_copies(step, h):
            copy.wait()
        above, below = min_[step, h, 0], min_[step, h, 1]
        return jnp.concatenate(
            [
                jnp.where(first, above, pltpu.roll(below, half, 1)),
                jnp.where(first, pltpu.roll(above, half, 1), below),
            ],
            axis=0,
        )

    def inserted(came, table):
        high, low = split(came)
        return dot_nt(high, table) + dot_nt(low, table)

    def send_gather(step, g, buf):
        fill = cfill[step, pl.ds(g, 1), :]
        for sub in range(quota // SUB):
            at = slice(sub * SUB, (sub + 1) * SUB)
            got = gather(csend[step, pl.ds(g, 1), at])
            for c in range(3):
                buf[c : c + 1, at] = got[c]
        for b in range(quota // LANES):
            live = lane < fill[:, b : b + 1]
            buf[3:4, b * LANES : (b + 1) * LANES] = jnp.where(live, 1.0, 0.0)

    def arrived_gather(step, g, moving, buf):
        for sub in range(quota // SUB):
            at = slice(sub * SUB, (sub + 1) * SUB)
            slot, node = locate(csend[step, pl.ds(g, 1), at])
            wide = jnp.concatenate([cross_col[...]] * (SUB // LANES), axis=1)
            table = jnp.where(wide == slot, 1.0, 0.0).astype(BF16)
            got = at_nodes(dot(moving, jnp.concatenate([table, table], axis=0)), node)
            for c in range(3):
                buf[c : c + 1, at] = ahead[g, c : c + 1, at] + got[c]
        buf[3:4, :] = ahead[g, 3:4, :]

    for copy in loads[:3]:
        copy.wait()
    set_parts(jnp.concatenate([state[c] for c in range(3)], axis=0))

    for step in range(STEPS):
        if step == 0:
            send_gather(step, i, rbuf.at[step, i])
            pl.semaphore_wait(barrier, groups + 1)

            @pl.loop(0, groups - 1)
            def _(k):
                to = mod(i + 1 + k)
                send_gather(step, to, sbuf.at[step, to])
                pair_copy(step, k).start()

        else:

            @pl.loop(0, groups - 1)
            def _(k):
                to = mod(i + 1 + k)
                arrived_gather(step, to, moving[...], sbuf.at[step, to])
                pair_copy(step, k).start()

            arrived_gather(step, i, moving[...], rbuf.at[step, i])
            set_parts(base[...] + inserted(came_nodes, cross_hot[step - 1]))

        if step == 0:
            for copy in loads[3:]:
                copy.wait()
            cross_hot = [slot_hot(crossing[s : s + 1, :], cross) for s in range(STEPS)]
            ones = jnp.ones((16, cross), BF16)
            keeps = [1.0 - dot_nt(ones, t)[:1] for t in cross_hot]
            coef = coef0[...]
            wide_coef = jnp.broadcast_to(coef, (16, fdev))
            leaving = sum(dot(p, cross_hot[0]) for p in split3(wide_coef))
            coef_out[...] = leaving[:8]
            coef_copies = [
                pltpu.make_async_remote_copy(
                    src_ref=coef_out, dst_ref=coef_in.at[d],
                    send_sem=c_send.at[d], recv_sem=c_recv.at[d],
                    device_id=dev, device_id_type=MESH,
                )
                for d, dev in enumerate((down_dev, up_dev))
            ]
            for copy in coef_copies:
                copy.start()
            set_scale(coef)
            for c in range(3, fields):
                xh[c * nodes : (c + 1) * nodes, :] = forward(state[c]) * scale[...]
            leave(step, 1, xh[rot_at, :], cross_hot[step])

        column = jnp.broadcast_to(crossing[step : step + 1, :].astype(F32), (LANES, cross))
        cross_col[...] = column.T.astype(jnp.int32)

        @pl.loop(0, groups)
        def _(g):
            for sub in range(quota // SUB):
                at = slice(sub * SUB, (sub + 1) * SUB)
                index = crecv[step, pl.ds(g, 1), at]
                wide = jnp.concatenate([cross_col[...]] * (SUB // LANES), axis=1)
                same = wide == locate(index)[0]
                hotx[g, :, at] = jnp.where(same, 1.0, 0.0).astype(BF16)
                got = gather(index, g, sub)
                for c in range(3):
                    local[g, c : c + 1, at] = got[c]

        if step == 0:
            for c in range(3):
                xh[c * nodes : (c + 1) * nodes, :] = forward(state[c])
        else:
            for copy in coef_copies:
                copy.wait()
            arrived = jnp.where(
                lax.broadcasted_iota(jnp.int32, (8, cross), 1) < half,
                coef_in[0], coef_in[1],
            )
            arrived = jnp.concatenate([arrived, arrived], axis=0)
            moved = sum(dot_nt(p, cross_hot[0]) for p in split3(arrived))
            coef = coef * keeps[0] + moved[:1]
            wide_coef = jnp.broadcast_to(coef, (16, fdev))
            leaving = sum(dot(p, cross_hot[step]) for p in split3(wide_coef))
            set_scale(coef)
            xh[pos_at, :] = xh[pos_at, :] * keeps[0] + inserted(came, cross_hot[0])
            turned = inserted(arrive(0, 1), cross_hot[0])
            for c in range(3):
                at = slice(npos + c * nodes, npos + (c + 1) * nodes)
                moved_in = turned[c * nodes : (c + 1) * nodes]
                xh[at, :] = (xh[at, :] * keeps[0] + moved_in) * scale[...]
            leave(step, 1, xh[rot_at, :], cross_hot[step])

        lead[...] = pick(xh[pos_at, :], cross_hot[step])
        scale_x = 1.0 / (1.0 + lam[...] * leaving[:1])
        accx[...] = jnp.zeros_like(accx)

        def scatter(g):
            delta = rbuf[step, g, 0:3] - local[g, 0:3]
            radius = jnp.sum(delta * delta, axis=0, keepdims=True)
            live = rbuf[step, g, 3:4] > 0.5
            force = jnp.where(live, 0.5 * delta / (1.0 + radius), 0.0)
            node = locate(crecv[step, pl.ds(g, 1), :])[1].astype(F32)
            wide = jnp.concatenate([iota[:nodes]] * (quota // LANES), axis=1)
            node_hot = jnp.where(wide == tall(node, nodes), BF16(1), BF16(0))
            high, low = split(force)
            spread = [
                node_hot * tall(p[c : c + 1].astype(F32), nodes)
                for p in (high, low)
                for c in range(3)
            ]
            spread = jnp.concatenate(spread, axis=0)
            spreads[g] = spread
            accx[...] += dot_nt(spread, hotx[g])

        scatter(i)

        @pl.loop(0, groups - 1)
        def _(k):
            source = mod(i + groups - 1 - k)
            pair_arrival(step, source).wait_recv()
            scatter(source)

        def pushed(total, c):
            at = slice(c * nodes, (c + 1) * nodes)
            low_at = slice(npos + c * nodes, npos + (c + 1) * nodes)
            return at, forward(total[at, :] + total[low_at, :])

        leavers = []
        for c in range(3):
            at, push = pushed(accx, c)
            leavers.append((lead[at, :] + push) * scale_x)
        send_off(step, 0, jnp.concatenate(leavers, axis=0))

        acc[...] = jnp.zeros_like(acc)

        @pl.loop(0, groups)
        def _(g):
            acc[...] += dot_nt(spreads[g], hot[g])

        for c in range(3):
            at, push = pushed(acc, c)
            xh[at, :] = (xh[at, :] + push) * scale[...]
        table, keep = cross_hot[step], keeps[step]

        base[...] = backward(xh[pos_at, :] * keep)
        if step < STEPS - 1:
            set_parts(base[...])

            @pl.loop(0, groups)
            def _(g):
                send_gather(step + 1, g, ahead.at[g])

            came = arrive(step, 0)
            came_nodes = backward(came)
            moving[...] = jnp.concatenate(split(came_nodes), axis=1)
        else:
            turned = backward(xh[rot_at, :] * keep)
            turned += inserted(backward(arrive(step, 1)), table)
            for c in range(3):
                out[3 + c] = turned[c * nodes : (c + 1) * nodes]
            placed = base[...] + inserted(backward(arrive(step, 0)), table)
            for c in range(3):
                out[c] = placed[c * nodes : (c + 1) * nodes]

    for step in range(STEPS):

        @pl.loop(0, groups - 1)
        def _(k):
            pair_copy(step, k).wait_send()


def per_device(groups, n_stream, state, stiffness, crossing, csend, crecv, cfill):
    fields, nodes, fdev = state.shape
    quota = csend.shape[2]
    cross = crossing.shape[1]
    rows = fields * nodes
    fwd, inv, lam = cosine_tables(nodes)
    mats = np.concatenate([fwd, inv], axis=0).astype(np.float32)
    hbm = pl.BlockSpec(memory_space=pltpu.HBM)
    return pl.pallas_call(
        functools.partial(kernel, groups, n_stream),
        out_shape=pltpu.VMEM(state.shape, F32),
        in_specs=[hbm] * 8,
        out_specs=pl.BlockSpec(memory_space=pltpu.VMEM),
        scratch_shapes=[
            pltpu.VMEM(state.shape, F32),
            pltpu.VMEM((1, fdev), F32),
            pltpu.VMEM(crossing.shape, jnp.int32),
            pltpu.VMEM(csend.shape, jnp.int32),
            pltpu.VMEM(crecv.shape, jnp.int32),
            pltpu.VMEM(cfill.shape, jnp.int32),
            pltpu.VMEM(mats.shape, F32),
            pltpu.VMEM(lam.shape, F32),
            pltpu.VMEM((HALF_SLOTS, LANES), BF16),
            pltpu.VMEM((rows, fdev), F32),
            pltpu.VMEM((6 * nodes, fdev), BF16),
            pltpu.VMEM((groups, fdev, quota), BF16),
            pltpu.VMEM((groups, 4, quota), F32),
            pltpu.VMEM((6 * nodes, fdev), F32),
            pltpu.VMEM((nodes, fdev), F32),
            pltpu.VMEM((3 * nodes, fdev), F32),
            pltpu.VMEM((groups, 4, quota), F32),
            pltpu.VMEM((cross, LANES), jnp.int32),
            pltpu.VMEM((3 * nodes, 2 * cross), BF16),
            pltpu.VMEM((groups, cross, quota), BF16),
            pltpu.VMEM((groups, 6 * nodes, quota), BF16),
            pltpu.VMEM((3 * nodes, cross), F32),
            pltpu.VMEM((6 * nodes, cross), F32),
            pltpu.VMEM((2, 8, cross), F32),
            pltpu.VMEM((8, cross), F32),
            pltpu.VMEM((STEPS, groups, 4, quota), F32),
            pltpu.VMEM((STEPS, groups, 4, quota), F32),
            pltpu.VMEM((STEPS, 2, 2, rows // 4, cross), F32),
            pltpu.VMEM((STEPS, 2, 2, rows // 4, cross), F32),
            pltpu.SemaphoreType.DMA((9,)),
            pltpu.SemaphoreType.DMA((2,)),
            pltpu.SemaphoreType.DMA((2,)),
            pltpu.SemaphoreType.DMA((STEPS, groups)),
            pltpu.SemaphoreType.DMA((STEPS, groups)),
            pltpu.SemaphoreType.DMA((STEPS, 2, 2)),
            pltpu.SemaphoreType.DMA((STEPS, 2, 2)),
        ],
        compiler_params=pltpu.CompilerParams(
            collective_id=0, has_side_effects=True, vmem_limit_bytes=40 * 2**20
        ),
    )(
        *(
            pltpu.with_memory_space_constraint(x, pltpu.HBM)
            for x in (
                state, stiffness.reshape(1, fdev), crossing, csend, crecv, cfill,
                jnp.asarray(mats), jnp.asarray(lam),
            )
        )
    )


def solution(mesh):
    cells = ("span", "stream")
    placed = (
        P(None, None, cells),
        P(cells),
        P(None, cells),
        P(None, None, cells),
        P(None, None, cells),
        P(None, None, cells),
    )
    return jax.shard_map(
        functools.partial(per_device, mesh.shape["span"], mesh.shape["stream"]),
        mesh=mesh,
        in_specs=placed,
        out_specs=P(None, None, cells),
        check_vma=False,
    )
```

```python
import functools
import math

import jax
import jax.numpy as jnp
import ml_dtypes
import numpy as np
from jax import lax
from jax.experimental import pallas as pl
from jax.experimental.pallas import tpu as pltpu
from jax.sharding import PartitionSpec as P

STEPS = 2
MESH = pl.DeviceIdType.MESH
F32 = jnp.float32
BF16 = jnp.bfloat16
LANES = 128
HALF_SLOTS = 256
SUB = 256
BY_LANES = 1


def cosine_tables(nodes):
    k = np.arange(nodes)[:, None]
    n = np.arange(nodes)[None, :]
    basis = np.sqrt(2.0 / nodes) * np.cos(np.pi * (n + 0.5) * k / nodes)
    basis[0] /= math.sqrt(2.0)

    def stacked(matrix):
        high = matrix.astype(ml_dtypes.bfloat16)
        low = (matrix - high.astype(np.float64)).astype(ml_dtypes.bfloat16)
        return np.concatenate([high, high, low, np.zeros_like(low)], axis=1)

    lam = 2.0 - 2.0 * np.cos(np.pi * np.arange(nodes) / nodes)
    lam = np.repeat(lam[:, None], LANES, axis=1).astype(np.float32)
    return stacked(basis), stacked(basis.T), lam


def split(x):
    high = x.astype(BF16)
    return high, (x - high.astype(F32)).astype(BF16)


def split3(x):
    high, rest = x.astype(BF16), None
    rest = x - high.astype(F32)
    mid = rest.astype(BF16)
    return high, mid, (rest - mid.astype(F32)).astype(BF16)


def dot(a, b):
    return jnp.dot(a, b, preferred_element_type=F32)


def dot_nt(a, b):
    return lax.dot_general(a, b, (((1,), (1,)), ((), ())), preferred_element_type=F32)


def along_nodes(matrix, block):
    high, low = split(block)
    return dot(matrix, jnp.concatenate([high, low, high], axis=0))


def tall(row, rows):
    tile = jnp.broadcast_to(row, (16, row.shape[1])).astype(BF16)
    return jnp.concatenate([tile] * (rows // 16), axis=0)


def kernel(
    groups, n_stream,
    state_hbm, coef_hbm, crossing_hbm, csend_hbm, crecv_hbm, cfill_hbm, mats_hbm, lam_hbm,
    out,
    state, coef0, crossing, csend, crecv, cfill, mats, lam, iota,
    xh, parts, exact, hot, local, acc, scale, base, ahead, cross_col, moving, coef_in, coef_out, sbuf, rbuf, mout, min_,
    l_sem, c_send, c_recv, p_send, p_recv, m_send, m_recv,
):
    fields, nodes, fdev = state.shape
    quota = csend.shape[2]
    cross = crossing.shape[1]
    half = cross // 2
    npos = 3 * nodes
    i = lax.axis_index("span")
    j = lax.axis_index("stream")
    down_dev = (i, lax.rem(j + 1, n_stream))
    up_dev = (i, lax.rem(j + n_stream - 1, n_stream))
    pos_at, rot_at = slice(0, npos), slice(npos, 2 * npos)

    def mod(v):
        return lax.rem(v, groups)

    barrier = pltpu.get_barrier_semaphore()
    for dev in (down_dev, up_dev):
        pl.semaphore_signal(barrier, inc=1, device_id=dev, device_id_type=MESH)
    for k in range(1, groups):
        pl.semaphore_signal(
            barrier, inc=1, device_id=(mod(i + k), j), device_id_type=MESH
        )

    moves = [
        (state_hbm.at[0:3], state.at[0:3]),
        (csend_hbm, csend),
        (cfill_hbm, cfill),
        (crecv_hbm, crecv),
        (crossing_hbm, crossing),
        (coef_hbm, coef0),
        (mats_hbm, mats),
        (lam_hbm, lam),
        (state_hbm.at[3:6], state.at[3:6]),
    ]
    loads = [
        pltpu.make_async_copy(src, dst, l_sem.at[n])
        for n, (src, dst) in enumerate(moves)
    ]
    for copy in loads:
        copy.start()

    iota[...] = (
        lax.broadcasted_iota(jnp.int32, (HALF_SLOTS, LANES), 0).astype(F32).astype(BF16)
    )
    lane = lax.broadcasted_iota(jnp.int32, (1, LANES), 1)
    node_iota = lax.broadcasted_iota(jnp.int32, (nodes, SUB), 0)

    def slot_hot(slot, q):
        pieces = []
        for part in range(fdev // HALF_SLOTS):
            rel = slot - part * HALF_SLOTS
            inside = (rel >= 0) & (rel < HALF_SLOTS)
            val = jnp.where(inside, rel, -1).astype(F32)
            wide = jnp.concatenate([iota[...]] * (q // LANES), axis=1)
            same = wide == tall(val, HALF_SLOTS)
            pieces.append(jnp.where(same, BF16(1), BF16(0)))
        return jnp.concatenate(pieces, axis=0)

    def locate(index):
        if fdev & (fdev - 1) == 0:
            return index & (fdev - 1), index >> (fdev.bit_length() - 1)
        return lax.rem(index, fdev), lax.div(index, fdev)

    def gather(index, keep_at=None, sub=0):
        slot, node = locate(index)
        table = slot_hot(slot, SUB)
        if keep_at is not None:
            hot[keep_at, :, sub * SUB : (sub + 1) * SUB] = table
        picked = dot(parts[...], table)
        return at_nodes(picked[:npos] + picked[npos:], node)

    def lane_gather(index):
        slot, node = locate(index)
        at_lane = jnp.broadcast_to(slot & (LANES - 1), (npos, LANES))
        block = jnp.broadcast_to(slot >> 7, (npos, LANES))
        picked = jnp.zeros((npos, LANES), F32)
        for b in range(fdev // LANES):
            part = jnp.take_along_axis(
                exact[:, b * LANES : (b + 1) * LANES], at_lane, axis=1,
                mode="promise_in_bounds",
            )
            picked = jnp.where(block == b, part, picked)
        return at_nodes(picked, node)

    def gather_group(indices, step, g, buf, keep_at=None):
        subs = quota // SUB
        for sub in range(subs):
            at = slice(sub * SUB, (sub + 1) * SUB)
            index = indices[step, pl.ds(g, 1), at]
            if sub < subs - BY_LANES:
                got = gather(index, keep_at, sub)
                for c in range(3):
                    buf[c : c + 1, at] = got[c]
                continue
            if keep_at is not None:
                hot[keep_at, :, at] = slot_hot(locate(index)[0], SUB)
            for n in range(SUB // LANES):
                piece = slice(n * LANES, (n + 1) * LANES)
                to = slice(sub * SUB + n * LANES, sub * SUB + (n + 1) * LANES)
                got = lane_gather(index[:, piece])
                for c in range(3):
                    buf[c : c + 1, to] = got[c]

    def at_nodes(picked, node):
        mask = node_iota[:, : node.shape[1]] == node
        return [
            jnp.sum(
                jnp.where(mask, picked[c * nodes : (c + 1) * nodes], 0.0),
                axis=0, keepdims=True,
            )
            for c in range(3)
        ]

    def set_parts(block):
        high, low = split(block)
        parts[:npos, :] = high
        parts[npos:, :] = low
        exact[...] = block

    def forward(block):
        return along_nodes(mats[:nodes, : 3 * nodes].astype(BF16), block)

    def backward(block):
        back = mats[nodes:, : 3 * nodes].astype(BF16)
        return jnp.concatenate(
            [along_nodes(back, block[c * nodes : (c + 1) * nodes]) for c in range(3)],
            axis=0,
        )

    def set_scale(c):
        for b in range(fdev // LANES):
            at = slice(b * LANES, (b + 1) * LANES)
            scale[:, at] = 1.0 / (1.0 + lam[...] * c[:, at])

    def pair_copy(step, k):
        to = mod(i + 1 + k)
        return pltpu.make_async_remote_copy(
            src_ref=sbuf.at[step, to], dst_ref=rbuf.at[step, i],
            send_sem=p_send.at[step, to], recv_sem=p_recv.at[step, i],
            device_id=(to, j), device_id_type=MESH,
        )

    def pair_arrival(step, source):
        return pltpu.make_async_remote_copy(
            src_ref=sbuf.at[step, source], dst_ref=rbuf.at[step, source],
            send_sem=p_send.at[step, source], recv_sem=p_recv.at[step, source],
            device_id=(source, j), device_id_type=MESH,
        )

    first = lax.broadcasted_iota(jnp.int32, (npos // 2, cross), 1) < half

    def fibre_copies(step, h):
        return [
            pltpu.make_async_remote_copy(
                src_ref=mout.at[step, h, d], dst_ref=min_.at[step, h, d],
                send_sem=m_send.at[step, h, d], recv_sem=m_recv.at[step, h, d],
                device_id=dev, device_id_type=MESH,
            )
            for d, dev in enumerate((down_dev, up_dev))
        ]

    def leave(step, h, block, table):
        high, low = split(block)
        picked = dot(high, table) + dot(low, table)
        top, bottom = picked[: npos // 2], picked[npos // 2 :]
        mout[step, h, 0] = jnp.where(first, top, pltpu.roll(bottom, half, 1))
        mout[step, h, 1] = jnp.where(first, pltpu.roll(top, half, 1), bottom)
        for copy in fibre_copies(step, h):
            copy.start()

    def arrive(step, h):
        for copy in fibre_copies(step, h):
            copy.wait()
        above, below = min_[step, h, 0], min_[step, h, 1]
        return jnp.concatenate(
            [
                jnp.where(first, above, pltpu.roll(below, half, 1)),
                jnp.where(first, pltpu.roll(above, half, 1), below),
            ],
            axis=0,
        )

    def inserted(came, table):
        high, low = split(came)
        return dot_nt(high, table) + dot_nt(low, table)

    def send_gather(step, g, buf):
        fill = cfill[step, pl.ds(g, 1), :]
        gather_group(csend, step, g, buf)
        for b in range(quota // LANES):
            live = lane < fill[:, b : b + 1]
            buf[3:4, b * LANES : (b + 1) * LANES] = jnp.where(live, 1.0, 0.0)

    def arrived_gather(step, g, moving, buf):
        for sub in range(quota // SUB):
            at = slice(sub * SUB, (sub + 1) * SUB)
            slot, node = locate(csend[step, pl.ds(g, 1), at])
            wide = jnp.concatenate([cross_col[...]] * (SUB // LANES), axis=1)
            table = jnp.where(wide == slot, 1.0, 0.0).astype(BF16)
            got = at_nodes(dot(moving, jnp.concatenate([table, table], axis=0)), node)
            for c in range(3):
                buf[c : c + 1, at] = ahead[g, c : c + 1, at] + got[c]
        buf[3:4, :] = ahead[g, 3:4, :]

    for copy in loads[:3]:
        copy.wait()
    set_parts(jnp.concatenate([state[c] for c in range(3)], axis=0))

    for step in range(STEPS):
        if step == 0:
            send_gather(step, i, rbuf.at[step, i])
            pl.semaphore_wait(barrier, groups + 1)

            @pl.loop(0, groups - 1)
            def _(k):
                to = mod(i + 1 + k)
                send_gather(step, to, sbuf.at[step, to])
                pair_copy(step, k).start()

        else:

            @pl.loop(0, groups - 1)
            def _(k):
                to = mod(i + 1 + k)
                arrived_gather(step, to, moving[...], sbuf.at[step, to])
                pair_copy(step, k).start()

            arrived_gather(step, i, moving[...], rbuf.at[step, i])
            set_parts(base[...] + inserted(came_nodes, cross_hot[step - 1]))

        if step == 0:
            for copy in loads[3:]:
                copy.wait()
            cross_hot = [slot_hot(crossing[s : s + 1, :], cross) for s in range(STEPS)]
            ones = jnp.ones((16, cross), BF16)
            keeps = [1.0 - dot_nt(ones, t)[:1] for t in cross_hot]
            coef = coef0[...]
            wide_coef = jnp.broadcast_to(coef, (16, fdev))
            leaving = sum(dot(p, cross_hot[0]) for p in split3(wide_coef))
            coef_out[...] = leaving[:8]
            coef_copies = [
                pltpu.make_async_remote_copy(
                    src_ref=coef_out, dst_ref=coef_in.at[d],
                    send_sem=c_send.at[d], recv_sem=c_recv.at[d],
                    device_id=dev, device_id_type=MESH,
                )
                for d, dev in enumerate((down_dev, up_dev))
            ]
            for copy in coef_copies:
                copy.start()
            set_scale(coef)
            for c in range(3, fields):
                xh[c * nodes : (c + 1) * nodes, :] = forward(state[c]) * scale[...]
            leave(step, 1, xh[rot_at, :], cross_hot[step])

        @pl.loop(0, groups)
        def _(g):
            gather_group(crecv, step, g, local.at[g], g)

        if step == 0:
            for c in range(3):
                xh[c * nodes : (c + 1) * nodes, :] = forward(state[c])
        else:
            for copy in coef_copies:
                copy.wait()
            arrived = jnp.where(
                lax.broadcasted_iota(jnp.int32, (8, cross), 1) < half,
                coef_in[0], coef_in[1],
            )
            arrived = jnp.concatenate([arrived, arrived], axis=0)
            moved = sum(dot_nt(p, cross_hot[0]) for p in split3(arrived))
            set_scale(coef * keeps[0] + moved[:1])
            xh[pos_at, :] = xh[pos_at, :] * keeps[0] + inserted(came, cross_hot[0])
            turned = inserted(arrive(0, 1), cross_hot[0])
            for c in range(3):
                at = slice(npos + c * nodes, npos + (c + 1) * nodes)
                moved_in = turned[c * nodes : (c + 1) * nodes]
                xh[at, :] = (xh[at, :] * keeps[0] + moved_in) * scale[...]
            leave(step, 1, xh[rot_at, :], cross_hot[step])

        acc[...] = jnp.zeros_like(acc)

        def scatter(g):
            delta = rbuf[step, g, 0:3] - local[g, 0:3]
            radius = jnp.sum(delta * delta, axis=0, keepdims=True)
            live = rbuf[step, g, 3:4] > 0.5
            force = jnp.where(live, 0.5 * delta / (1.0 + radius), 0.0)
            node = locate(crecv[step, pl.ds(g, 1), :])[1].astype(F32)
            wide = jnp.concatenate([iota[:nodes]] * (quota // LANES), axis=1)
            node_hot = jnp.where(wide == tall(node, nodes), BF16(1), BF16(0))
            high, low = split(force)
            spread = [
                node_hot * tall(p[c : c + 1].astype(F32), nodes)
                for p in (high, low)
                for c in range(3)
            ]
            acc[...] += dot_nt(jnp.concatenate(spread, axis=0), hot[g])

        scatter(i)

        @pl.loop(0, groups - 1)
        def _(k):
            source = mod(i + groups - 1 - k)
            pair_arrival(step, source).wait_recv()
            scatter(source)

        for c in range(3):
            at = slice(c * nodes, (c + 1) * nodes)
            low_at = slice(npos + c * nodes, npos + (c + 1) * nodes)
            push = forward(acc[at, :] + acc[low_at, :])
            xh[at, :] = (xh[at, :] + push) * scale[...]
        table, keep = cross_hot[step], keeps[step]
        leave(step, 0, xh[pos_at, :], table)

        base[...] = backward(xh[pos_at, :] * keep)
        if step < STEPS - 1:
            set_parts(base[...])
            column = jnp.broadcast_to(crossing[step : step + 1, :].astype(F32), (LANES, cross))
            cross_col[...] = column.T.astype(jnp.int32)

            @pl.loop(0, groups)
            def _(g):
                send_gather(step + 1, g, ahead.at[g])

            came = arrive(step, 0)
            came_nodes = backward(came)
            moving[...] = jnp.concatenate(split(came_nodes), axis=1)
        else:
            turned = backward(xh[rot_at, :] * keep)
            turned += inserted(backward(arrive(step, 1)), table)
            for c in range(3):
                out[3 + c] = turned[c * nodes : (c + 1) * nodes]
            placed = base[...] + inserted(backward(arrive(step, 0)), table)
            for c in range(3):
                out[c] = placed[c * nodes : (c + 1) * nodes]

    for step in range(STEPS):

        @pl.loop(0, groups - 1)
        def _(k):
            pair_copy(step, k).wait_send()


def per_device(groups, n_stream, state, stiffness, crossing, csend, crecv, cfill):
    fields, nodes, fdev = state.shape
    quota = csend.shape[2]
    cross = crossing.shape[1]
    rows = fields * nodes
    fwd, inv, lam = cosine_tables(nodes)
    mats = np.concatenate([fwd, inv], axis=0).astype(np.float32)
    hbm = pl.BlockSpec(memory_space=pltpu.HBM)
    return pl.pallas_call(
        functools.partial(kernel, groups, n_stream),
        out_shape=pltpu.VMEM(state.shape, F32),
        in_specs=[hbm] * 8,
        out_specs=pl.BlockSpec(memory_space=pltpu.VMEM),
        scratch_shapes=[
            pltpu.VMEM(state.shape, F32),
            pltpu.VMEM((1, fdev), F32),
            pltpu.VMEM(crossing.shape, jnp.int32),
            pltpu.VMEM(csend.shape, jnp.int32),
            pltpu.VMEM(crecv.shape, jnp.int32),
            pltpu.VMEM(cfill.shape, jnp.int32),
            pltpu.VMEM(mats.shape, F32),
            pltpu.VMEM(lam.shape, F32),
            pltpu.VMEM((HALF_SLOTS, LANES), BF16),
            pltpu.VMEM((rows, fdev), F32),
            pltpu.VMEM((6 * nodes, fdev), BF16),
            pltpu.VMEM((3 * nodes, fdev), F32),
            pltpu.VMEM((groups, fdev, quota), BF16),
            pltpu.VMEM((groups, 4, quota), F32),
            pltpu.VMEM((6 * nodes, fdev), F32),
            pltpu.VMEM((nodes, fdev), F32),
            pltpu.VMEM((3 * nodes, fdev), F32),
            pltpu.VMEM((groups, 4, quota), F32),
            pltpu.VMEM((cross, LANES), jnp.int32),
            pltpu.VMEM((3 * nodes, 2 * cross), BF16),
            pltpu.VMEM((2, 8, cross), F32),
            pltpu.VMEM((8, cross), F32),
            pltpu.VMEM((STEPS, groups, 4, quota), F32),
            pltpu.VMEM((STEPS, groups, 4, quota), F32),
            pltpu.VMEM((STEPS, 2, 2, rows // 4, cross), F32),
            pltpu.VMEM((STEPS, 2, 2, rows // 4, cross), F32),
            pltpu.SemaphoreType.DMA((9,)),
            pltpu.SemaphoreType.DMA((2,)),
            pltpu.SemaphoreType.DMA((2,)),
            pltpu.SemaphoreType.DMA((STEPS, groups)),
            pltpu.SemaphoreType.DMA((STEPS, groups)),
            pltpu.SemaphoreType.DMA((STEPS, 2, 2)),
            pltpu.SemaphoreType.DMA((STEPS, 2, 2)),
        ],
        compiler_params=pltpu.CompilerParams(
            collective_id=0, has_side_effects=True, vmem_limit_bytes=40 * 2**20
        ),
    )(
        *(
            pltpu.with_memory_space_constraint(x, pltpu.HBM)
            for x in (
                state, stiffness.reshape(1, fdev), crossing, csend, crecv, cfill,
                jnp.asarray(mats), jnp.asarray(lam),
            )
        )
    )


def solution(mesh):
    cells = ("span", "stream")
    placed = (
        P(None, None, cells),
        P(cells),
        P(None, cells),
        P(None, None, cells),
        P(None, None, cells),
        P(None, None, cells),
    )
    return jax.shard_map(
        functools.partial(per_device, mesh.shape["span"], mesh.shape["stream"]),
        mesh=mesh,
        in_specs=placed,
        out_specs=P(None, None, cells),
        check_vma=False,
    )
```
